256 devices in a mesh: dom: 64 (over y, z, core), sub: 4 (over x).
Axes of the slice: x: 4, y: 4, z: 8, core: 2. Of those that a mesh axis runs over, the one named last changes fastest.
Arguments:
- dofs: float32 [35, 9, 32768], P(None, None, ('dom', 'sub')), may hold values from -6 to 6
- stiffness: float32 [3, 35, 35], replicated
- star: float32 [3, 9, 9, 32768], P(None, None, None, ('dom', 'sub'))
- local_flux: float32 [4, 9, 9, 32768], P(None, None, None, ('dom', 'sub'))
- neighbour_flux: float32 [4, 9, 9, 32768], P(None, None, None, ('dom', 'sub'))
- face_proj: float32 [4, 15, 35], replicated, may hold values from -1 to 1
- face_rot: float32 [3, 15, 15], replicated
- cluster: int32 [32768], P(('dom', 'sub')), may hold values from 0 to 3, as said below
- neighbour: int32 [4, 32768], P(None, ('dom', 'sub')), may hold values from 0 to 896, as said below
- orient: int32 [4, 32768], P(None, ('dom', 'sub')), may hold values from 0 to 2
- send_list: int32 [64, 4, 96], P('dom', 'sub'), may hold values from 0 to 512, as said below
Outputs:
- dofs_out: float32 [35, 9, 32768], P(None, None, ('dom', 'sub'))
The draws below stay inside these ranges and needn't reach their ends.
Inputs may be any that keep to these rules, and one draw needn't show every extreme that they name: Along a device's 128 elements the cluster ids never fall. On every device clusters 0, 1 and 2 hold at most 32 elements each, and for each of the three some device holds exactly that many. `send_list`: entry (b * 4 + t) * 8 + l of a device's list names the face j * 128 + n (face j of its element n) whose data go to the device b - 1 steps further along dom at sub index t, in slot l of that link; 512 marks an empty slot. The live slots of a link come first, both ends of a link use the same number of slots, and some link fills all 8. No slot leads past an end of dom or to the device itself. For face i of element n on a device: a code c below 512 names face c // 128 of element c % 128 on the same device; a code 4 * 128 + 4 k + f names face f of the element held by slot k of the data that reach the device, where k = (b * 4 + t) * 8 + l is slot l of the link from the device at sub index t that lies b - 1 steps lower along dom; 896 marks a boundary face. Faces neighbour each other in pairs.
All inputs are finite; a program needn't handle non-finite values.
Results may differ from the reference program's by a relative error of at most 0.0001.
Values sent between devices are 32-bit elements; how exact they have to be, the bound alone decides.
No kernel may reach another device: no remote copies, remote signals or barrier semaphores. Data moves between devices by JAX's collectives and lax.ppermute only.
A program may use at most 192 MiB of HBM per device.

```python
import jax
import jax.numpy as jnp
from jax import lax

NB = 35
NF = 15
NV = 9
ORDER = 5
STEPS = 8
E_DEV = 128
H = 8
ELEMS = 32768
N_DOM = 64
N_SUB = 4


def mesh_tables(key):
    devices_n = N_DOM * N_SUB
    face_total = 4 * E_DEV
    slot_count = 3 * N_SUB * H
    key_up, key_side, key_perm, key_pick = jax.random.split(key, 4)
    upward = jax.random.randint(key_up, (N_DOM, N_SUB, N_SUB), H // 4, H + 1)
    pick_keys = jax.random.split(key_pick, 3)
    pick_dom = jax.random.randint(pick_keys[0], (), 0, N_DOM - 1)
    pick_from = jax.random.randint(pick_keys[1], (), 0, N_SUB)
    pick_to = jax.random.randint(pick_keys[2], (), 0, N_SUB)
    upward = upward.at[pick_dom, pick_from, pick_to].set(H)
    dom_ids = jnp.arange(N_DOM)[:, None, None]
    upward = jnp.where(dom_ids < N_DOM - 1, upward, 0)
    downward = jnp.concatenate([jnp.zeros((1, N_SUB, N_SUB), jnp.int32), upward[:-1]], axis=0).transpose(0, 2, 1)
    raw_side = jax.random.randint(key_side, (N_DOM, N_SUB, N_SUB), H // 4, H + 1)
    from_ids = jnp.arange(N_SUB)[None, :, None]
    to_ids = jnp.arange(N_SUB)[None, None, :]
    sideways = jnp.where(from_ids < to_ids, raw_side, raw_side.transpose(0, 2, 1))
    sideways = jnp.where(from_ids == to_ids, 0, sideways)
    link_counts = jnp.stack([downward, sideways, upward], axis=2)
    live = jnp.arange(H)[None, None, None, None, :] < link_counts[..., None]
    live = live.reshape(devices_n, slot_count)
    perm_keys = jax.random.split(key_perm, devices_n)
    perms = jax.vmap(lambda one_key: jax.random.permutation(one_key, face_total))(perm_keys).astype(jnp.int32)
    send_codes = jnp.where(live, perms[:, :slot_count], face_total)
    live_all = jnp.concatenate([live, jnp.zeros((devices_n, face_total - slot_count), bool)], axis=1)
    order = jnp.argsort(jnp.where(live_all, 0, 1), axis=1, stable=True).astype(jnp.int32)
    live_total = jnp.sum(live.astype(jnp.int32), axis=1)[:, None]
    face_at = jnp.take_along_axis(perms, order, axis=1)
    ranks = jnp.arange(face_total, dtype=jnp.int32)[None, :]
    partner = live_total + jnp.bitwise_xor(ranks - live_total, 1)
    partner_face = jnp.take_along_axis(face_at, jnp.clip(partner, 0, face_total - 1), axis=1)
    local_code = jnp.where(partner < face_total, partner_face, face_total + 4 * slot_count)
    slot_pos = jnp.clip(order, 0, slot_count - 1)
    block_index = slot_pos // (N_SUB * H)
    target_sub = slot_pos // H % N_SUB
    link_slot = slot_pos % H
    device_ids = jnp.arange(devices_n, dtype=jnp.int32)[:, None]
    dom_index = device_ids // N_SUB
    sub_index = device_ids % N_SUB
    receive_slot = ((2 - block_index) * N_SUB + target_sub) * H + link_slot
    source_dev = jnp.clip(dom_index + block_index - 1, 0, N_DOM - 1) * N_SUB + target_sub
    source_slot = ((2 - block_index) * N_SUB + sub_index) * H + link_slot
    far_face = jnp.clip(send_codes[source_dev, source_slot], 0, face_total - 1) // E_DEV
    remote_code = face_total + 4 * receive_slot + far_face
    chosen = jnp.where(ranks < live_total, remote_code, local_code)
    neighbour_codes = jnp.zeros((devices_n, face_total), jnp.int32).at[device_ids, face_at].set(chosen)
    return (send_codes, neighbour_codes)


def draw_send_list(key, part):
    send_codes, unused_codes = mesh_tables(key)
    return send_codes.reshape(N_DOM, N_SUB, 3 * N_SUB * H).astype(jnp.int32)


def draw_neighbour(key, part):
    unused_codes, neighbour_codes = mesh_tables(key)
    shaped = neighbour_codes.reshape(N_DOM * N_SUB, 4, E_DEV).transpose(1, 0, 2)
    return shaped.reshape(4, ELEMS).astype(jnp.int32)


def draw_cluster(key, part):
    key = jax.random.fold_in(key, 5)
    key_sizes, key_force = jax.random.split(key)
    devices_n = N_DOM * N_SUB
    sizes = jax.random.randint(key_sizes, (devices_n, 3), E_DEV // 32, E_DEV // 4 + 1)
    forced = jax.random.randint(key_force, (3,), 0, devices_n)
    sizes = sizes.at[forced, jnp.arange(3)].set(E_DEV // 4)
    bounds = jnp.cumsum(sizes, axis=1)
    position = jnp.arange(E_DEV)[None, :]
    labels = jnp.zeros((devices_n, E_DEV), jnp.int32)
    for column in range(3):
        labels = labels + (position >= bounds[:, column:column + 1]).astype(jnp.int32)
    return labels.reshape(ELEMS).astype(jnp.int32)


def draw_stiffness(key, part):
    key = jax.random.fold_in(key, 7)
    key_raw, key_diag = jax.random.split(key)
    raw = jax.random.normal(key_raw, (3, NB, NB), jnp.float32) * 0.042
    skew = raw - raw.transpose(0, 2, 1)
    diagonal = jax.random.uniform(key_diag, (3, NB), jnp.float32, 0.03, 0.08)
    identity = jnp.arange(NB)[:, None] == jnp.arange(NB)[None, :]
    return jnp.where(identity[None], diagonal[:, :, None], skew).astype(jnp.float32)


def draw_star(key, part):
    key = jax.random.fold_in(key, 13)
    raw = jax.random.uniform(key, (3, NV, NV, ELEMS), jnp.float32, -1.0, 1.0)
    return ((raw + raw.transpose(0, 2, 1, 3)) * 0.5).astype(jnp.float32)


def draw_local_flux(key, part):
    key = jax.random.fold_in(key, 17)
    key_diag, key_off = jax.random.split(key)
    diagonal = jax.random.uniform(key_diag, (4, NV, ELEMS), jnp.float32, 0.1, 0.3)
    raw = jax.random.uniform(key_off, (4, NV, NV, ELEMS), jnp.float32, -0.012, 0.012)
    symmetric = (raw + raw.transpose(0, 2, 1, 3)) * 0.5
    identity = jnp.arange(NV)[:, None] == jnp.arange(NV)[None, :]
    return jnp.where(identity[None, :, :, None], diagonal[:, :, None, :], symmetric).astype(jnp.float32)


def draw_neighbour_flux(key, part):
    key = jax.random.fold_in(key, 19)
    key_diag, key_off = jax.random.split(key)
    diagonal = jax.random.uniform(key_diag, (4, NV, ELEMS), jnp.float32, 0.1, 0.3)
    raw = jax.random.uniform(key_off, (4, NV, NV, ELEMS), jnp.float32, -0.05, 0.05)
    identity = jnp.arange(NV)[:, None] == jnp.arange(NV)[None, :]
    return jnp.where(identity[None, :, :, None], diagonal[:, :, None, :], raw).astype(jnp.float32)


def draw_face_rot(key, part):
    key = jax.random.fold_in(key, 23)
    key_diag, key_off = jax.random.split(key)
    diagonal = jax.random.uniform(key_diag, (3, NF), jnp.float32, 0.8, 1.2)
    raw = jax.random.uniform(key_off, (3, NF, NF), jnp.float32, -0.15, 0.15)
    identity = jnp.arange(NF)[:, None] == jnp.arange(NF)[None, :]
    return jnp.where(identity[None], diagonal[:, :, None], raw).astype(jnp.float32)


def with_ends(drawn, key, smallest, top_value):
    spot = [jax.random.randint(jax.random.fold_in(key, axis), (), 0, length) for axis, length in enumerate(drawn.shape)]
    main_axis = drawn.shape.index(max(drawn.shape))
    next_to = spot[:main_axis] + [(spot[main_axis] + 1) % drawn.shape[main_axis]] + spot[main_axis + 1:]
    return drawn.at[tuple(spot)].set(smallest).at[tuple(next_to)].set(top_value)


def block_scale(own_key, extent, cuts, least, high):
    factor_of, own = 1.0, jax.random.fold_in(own_key, 6)
    for dim, parts in cuts:
        heights = jnp.exp(jax.random.uniform(jax.random.fold_in(own, dim), (parts,), jnp.float32, least / len(cuts), high / len(cuts)))
        factor_of = factor_of * jnp.repeat(heights, extent[dim] // parts).reshape([-1 if axis == dim else 1 for axis in range(len(extent))])
    return factor_of


def centred(stream_key, shape, spread, reach, shards=(), held_as=jnp.bfloat16):
    values = spread * jax.random.normal(stream_key, shape, jnp.float32)
    if shards:
        values = values * block_scale(stream_key, shape, shards, -0.22, 0.18)
    return jnp.clip(values, -reach, reach).astype(held_as)


def setup_inputs(seed: int = 0) -> dict:
    arg_keys = jax.random.split(jax.random.key(seed), 12)
    return {
        "dofs": centred(arg_keys[0], (NB, NV, ELEMS), 1.0, 6.0, ((2, 256),), jnp.float32),
        "stiffness": draw_stiffness(jax.random.fold_in(arg_keys[11], 71), 0),
        "star": draw_star(jax.random.fold_in(arg_keys[11], 71), 0),
        "local_flux": draw_local_flux(jax.random.fold_in(arg_keys[11], 71), 0),
        "neighbour_flux": draw_neighbour_flux(jax.random.fold_in(arg_keys[11], 71), 0),
        "face_proj": centred(arg_keys[5], (4, NF, NB), NB ** -0.5, 1.0, (), jnp.float32),
        "face_rot": draw_face_rot(jax.random.fold_in(arg_keys[11], 71), 0),
        "cluster": draw_cluster(jax.random.fold_in(arg_keys[11], 71), 0),
        "neighbour": draw_neighbour(jax.random.fold_in(arg_keys[11], 71), 0),
        "orient": with_ends(jax.random.randint(arg_keys[9], (4, ELEMS), 0, 3), jax.random.fold_in(arg_keys[9], 1), 0, 2).astype(jnp.int32),
        "send_list": draw_send_list(jax.random.fold_in(arg_keys[11], 71), 0),
    }


factorials = [1.0, 1.0, 2.0, 6.0, 24.0, 120.0, 720.0]


def star_apply(values, matrices):
    return jnp.einsum("bue,uve->bve", values, matrices, precision=lax.Precision.HIGHEST)


def taylor_terms(values, stiffness, star):
    levels = [values]
    current = values
    for degree in range(ORDER - 1):
        summed = jnp.zeros_like(current)
        for direction in range(3):
            applied = jnp.einsum("ab,bve->ave", stiffness[direction], current, precision=lax.Precision.HIGHEST)
            summed = summed - star_apply(applied, star[direction])
        current = summed
        levels.append(current)
    return jnp.stack(levels)


def substep_weights(substep, cluster):
    period = jnp.left_shift(jnp.int32(1), cluster)
    offset = (substep % period).astype(jnp.float32)
    step_scale = period.astype(jnp.float32)
    weights = []
    for degree in range(ORDER):
        upper = jnp.power(offset + 1.0, degree + 1) - jnp.power(offset, degree + 1)
        weights.append(upper / (jnp.power(step_scale, degree) * factorials[degree + 1]))
    return jnp.stack(weights)


def integrate(terms, weights):
    summed = terms[0] * weights[0]
    for degree in range(1, ORDER):
        summed = summed + terms[degree] * weights[degree]
    return summed


def element_update(own_integral, neighbour_sum, step_scale, stiffness, star, local_flux, neighbour_flux, face_proj, face_rot, orient):
    volume = jnp.zeros_like(own_integral)
    for direction in range(3):
        applied = jnp.einsum("ab,bve->ave", stiffness[direction], own_integral, precision=lax.Precision.HIGHEST)
        volume = volume - star_apply(applied, star[direction])
    volume = volume / step_scale
    own_faces = jnp.einsum("ifb,bve->ifve", face_proj, own_integral, precision=lax.Precision.HIGHEST)
    own_faces = jnp.einsum("ifue,iuve->ifve", own_faces, local_flux, precision=lax.Precision.HIGHEST)
    rotated = jnp.zeros_like(neighbour_sum)
    for orient_code in range(3):
        turned = jnp.einsum("gf,fvie->gvie", face_rot[orient_code], neighbour_sum, precision=lax.Precision.HIGHEST)
        rotated = rotated + jnp.where(orient == orient_code, turned, 0.0)
    far_faces = jnp.einsum("gvie,ivwe->igwe", rotated, neighbour_flux, precision=lax.Precision.HIGHEST)
    lifted = jnp.einsum("ifb,ifve->bve", face_proj, far_faces - own_faces, precision=lax.Precision.HIGHEST)
    return volume + lifted


def global_sources(neighbour, send_list):
    face_total = 4 * E_DEV
    slot_count = 3 * N_SUB * H
    element_ids = jnp.arange(ELEMS, dtype=jnp.int32)
    device_ids = element_ids // E_DEV
    dom_index = device_ids // N_SUB
    sub_index = device_ids % N_SUB
    local_face = neighbour // E_DEV
    local_index = local_face * ELEMS + device_ids * E_DEV + neighbour % E_DEV
    remote_code = jnp.clip(neighbour - face_total, 0, 4 * slot_count - 1)
    slot_index = remote_code // 4
    block_index = slot_index // (N_SUB * H)
    source_sub = (slot_index // H) % N_SUB
    link_slot = slot_index % H
    source_dom = jnp.clip(dom_index - block_index + 1, 0, N_DOM - 1)
    source_dev = source_dom * N_SUB + source_sub
    send_table = send_list.reshape(N_DOM * N_SUB, slot_count)
    sent_code = send_table[source_dev, (block_index * N_SUB + sub_index) * H + link_slot]
    sent_code = jnp.clip(sent_code, 0, face_total - 1)
    remote_index = (sent_code // E_DEV) * ELEMS + source_dev * E_DEV + sent_code % E_DEV
    boundary = neighbour >= face_total + 4 * slot_count
    chosen = jnp.where(neighbour < face_total, local_index, jnp.where(boundary, 4 * ELEMS, remote_index))
    return chosen.astype(jnp.int32)


def reference(dofs, stiffness, star, local_flux, neighbour_flux, face_proj, face_rot, cluster, neighbour, orient, send_list):
    sources = global_sources(neighbour, send_list)
    period = jnp.left_shift(jnp.int32(1), cluster)
    step_scale = period.astype(jnp.float32)
    solution = dofs
    terms = jnp.zeros((ORDER, NB, NV, ELEMS), jnp.float32)
    own_integral = jnp.zeros((NB, NV, ELEMS), jnp.float32)
    neighbour_sum = jnp.zeros((NF, NV, 4, ELEMS), jnp.float32)
    for substep in range(STEPS):
        starting = (substep % period) == 0
        terms = jnp.where(starting, taylor_terms(solution, stiffness, star), terms)
        integral = integrate(terms, substep_weights(substep, cluster))
        own_integral = own_integral + integral
        face_data = jnp.einsum("ifb,bve->fvie", face_proj, integral, precision=lax.Precision.HIGHEST).reshape(NF, NV, 4 * ELEMS)
        extended = jnp.concatenate([face_data, jnp.zeros((NF, NV, 1), jnp.float32)], axis=2)
        neighbour_sum = neighbour_sum + jnp.take(extended, sources, axis=2)
        finishing = ((substep + 1) % period) == 0
        change = element_update(own_integral, neighbour_sum, step_scale, stiffness, star, local_flux, neighbour_flux, face_proj, face_rot, orient)
        solution = jnp.where(finishing, solution + change, solution)
        own_integral = jnp.where(finishing, 0.0, own_integral)
        neighbour_sum = jnp.where(finishing, 0.0, neighbour_sum)
    return solution
```

```python
import functools

import jax
import jax.numpy as jnp
from jax import lax
from jax.experimental import pallas as pl
from jax.experimental.pallas import tpu as pltpu
from jax.sharding import PartitionSpec as P

ORDER = 5
STEPS = 8
NB = 35
NBP = 40
NBK = 48
NF = 15
NFP = 16
NV = 9
E = 128
H = 8
SLOTS = 96
FACES = 4 * E
WIDE = NV * NFP
COLS = NV * E
FACT = [1.0, 1.0, 2.0, 6.0, 24.0, 120.0, 720.0]
BF = jnp.bfloat16
F32 = jnp.float32


def halves(x):
    hi = x.astype(BF)
    lo = (x - hi.astype(F32)).astype(BF)
    return hi, lo


def dot(a, b):
    return jnp.dot(a, b, preferred_element_type=F32)


def fill_basis(xs_ref, values):
    pad = jnp.zeros((NBK - NBP, E), F32)
    for v in range(NV):
        hi, lo = halves(jnp.concatenate([values[v], pad], axis=0))
        cols = slice(v * E, (v + 1) * E)
        xs_ref[0:NBK, cols] = hi
        xs_ref[NBK : 2 * NBK, cols] = lo
        xs_ref[2 * NBK : 3 * NBK, cols] = hi


def derive(values, stiff_ref, star_ref, xs_ref):
    fill_basis(xs_ref, values)
    applied = dot(stiff_ref[...], xs_ref[...])
    acc = [None] * NV
    for d in range(3):
        for u in range(NV):
            part = applied[d * NBP : (d + 1) * NBP, u * E : (u + 1) * E]
            for v in range(NV):
                term = part * star_ref[d, u, v : v + 1, :]
                acc[v] = term if acc[v] is None else acc[v] + term
    return acc


def critical(first, last, step, *refs):
    refs = list(refs)
    take = lambda n: [refs.pop(0) for _ in range(n)]
    if first:
        (state_ref,) = take(1)
    else:
        rlo, rhi, g1, g2, g3, nsum_ref, base_ref, nflux, lift_a, lift_b, omask, far = take(12)
    if not last:
        stiff, star, proj, weights, pick = take(5)
        if not first:
            masks, terms_in = take(2)
    if last:
        (out_ref,) = take(1)
    else:
        if not first:
            (nsum_out,) = take(1)
        terms, d_hi, d_lo, pay_lo, pay_own, pay_hi = take(6)
    if not first:
        (xg,) = take(1)
    if not last:
        (xs,) = take(1)

    if first:
        upd = [state_ref[v] for v in range(NV)]
    else:
        empty = jnp.zeros((H, WIDE), F32)
        got = jnp.concatenate([rlo[0:H, :], empty, rhi[0:H, :], g1[...], g2[...], g3[...]], axis=0)
        got_hi, got_lo = halves(got)
        dims = (((0,), (0,)), ((), ()))
        arrived = lax.dot_general(got_hi, far[...], dims, preferred_element_type=F32)
        arrived = arrived + lax.dot_general(got_lo, far[...], dims, preferred_element_type=F32)
        total = nsum_ref[...] + arrived
        if not last:
            nsum_out[...] = total
        for i in range(4):
            acc = [None] * NV
            for u in range(NV):
                part = total[u * NFP : (u + 1) * NFP, i * E : (i + 1) * E]
                for v in range(NV):
                    term = part * nflux[i, u, v : v + 1, :]
                    acc[v] = term if acc[v] is None else acc[v] + term
            for v in range(NV):
                hi, lo = halves(acc[v])
                for o in range(3):
                    chosen = omask[i * 3 + o]
                    row = (i * 3 + o) * NFP
                    cols = slice(v * E, (v + 1) * E)
                    xg[row : row + NFP, cols] = hi * chosen
                    xg[192 + row : 192 + row + NFP, cols] = lo * chosen
        two = dot(lift_a[...], xg[0:192, :])
        lifted = two[0:NBP] + two[NBP : 2 * NBP] + dot(lift_b[...], xg[192:384, :])
        upd = [base_ref[v] + lifted[:, v * E : (v + 1) * E] for v in range(NV)]
        if last:
            for v in range(NV):
                out_ref[v] = upd[v][0:NB]
            return

    if not first:
        start = masks[step : step + 1, :] > 0.5
    current = upd
    total = [None] * NV
    for k in range(ORDER):
        if k > 0:
            current = derive(current, stiff, star, xs)
        for v in range(NV):
            kept = current[v] if first else jnp.where(start, current[v], terms_in[k, v])
            terms[k, v] = kept
            part = kept * weights[step * ORDER + k : step * ORDER + k + 1, :]
            total[v] = part if k == 0 else total[v] + part
    fill_basis(xs, total)
    faces = dot(proj[...], xs[...])
    for i in range(4):
        for v in range(NV):
            hi, lo = halves(faces[i * NFP : (i + 1) * NFP, v * E : (v + 1) * E])
            d_hi[v * NFP : (v + 1) * NFP, i * E : (i + 1) * E] = hi
            d_lo[v * NFP : (v + 1) * NFP, i * E : (i + 1) * E] = lo
    dims = (((1,), (1,)), ((), ()))
    pay = lax.dot_general(pick[...], d_hi[...], dims, preferred_element_type=F32)
    pay = pay + lax.dot_general(pick[...], d_lo[...], dims, preferred_element_type=F32)
    pay_lo[...] = pay[0:32]
    pay_own[...] = pay[32:64]
    pay_hi[...] = pay[64:96]


def beside(first, step, *refs):
    refs = list(refs)
    take = lambda n: [refs.pop(0) for _ in range(n)]
    terms, d_hi, d_lo, near, stiff, star, proj, lflux, own_lift, period = take(10)
    if not first:
        masks, nsum_ref, base_ref = take(3)
    nsum_out, base_out, xs, xq = take(4)
    gathered = dot(d_hi[...], near[...]) + dot(d_lo[...], near[...])
    if first:
        nsum_out[...] = gathered
    else:
        start = masks[step : step + 1, :]
        for i in range(4):
            cols = slice(i * E, (i + 1) * E)
            nsum_out[:, cols] = nsum_ref[:, cols] * (1.0 - start) + gathered[:, cols]
    final = derive([terms[ORDER - 1, v] for v in range(NV)], stiff, star, xs)
    state = []
    whole = []
    for v in range(NV):
        volume = final[v] * (1.0 / FACT[ORDER])
        own = terms[0, v]
        for k in range(1, ORDER):
            volume = volume + terms[k, v] * (1.0 / FACT[k])
            own = own + terms[k, v] * (1.0 / FACT[k + 1])
        state.append(terms[0, v] + volume)
        whole.append(own * period[0:1, :])
    fill_basis(xs, whole)
    faces = dot(proj[...], xs[...])
    for i in range(4):
        acc = [None] * NV
        for u in range(NV):
            part = faces[i * NFP : (i + 1) * NFP, u * E : (u + 1) * E]
            for v in range(NV):
                term = part * lflux[i, u, v : v + 1, :]
                acc[v] = term if acc[v] is None else acc[v] + term
        for v in range(NV):
            hi, lo = halves(acc[v])
            cols = slice(v * E, (v + 1) * E)
            xq[i * NFP : (i + 1) * NFP, cols] = hi
            xq[64 + i * NFP : 64 + (i + 1) * NFP, cols] = lo
            xq[128 + i * NFP : 128 + (i + 1) * NFP, cols] = hi
    lifted = dot(own_lift[...], xq[...])
    for v in range(NV):
        fresh = state[v] - lifted[:, v * E : (v + 1) * E]
        base_out[v] = fresh if first else jnp.where(start > 0.5, fresh, base_ref[v])


def call(kernel, outs, scratch, args):
    return pl.pallas_call(
        kernel,
        out_shape=[jax.ShapeDtypeStruct(s, t) for s, t in outs],
        in_specs=[pl.BlockSpec(memory_space=pltpu.VMEM)] * len(args),
        out_specs=[pl.BlockSpec(memory_space=pltpu.VMEM)] * len(outs),
        scratch_shapes=[pltpu.VMEM(s, t) for s, t in scratch],
        compiler_params=pltpu.CompilerParams(vmem_limit_bytes=40 * 1024 * 1024),
    )(*args)


def split(x):
    hi = lax.reduce_precision(x, 8, 7)
    return hi.astype(BF), (x - hi).astype(BF)


def stacked(x):
    hi, lo = split(x)
    return jnp.concatenate([hi, hi, lo], axis=1)


def body(dofs, stiffness, star, local_flux, neighbour_flux, face_proj, face_rot, cluster, neighbour, orient, send_list):
    sub = lax.axis_index("sub")
    high = lax.Precision.HIGHEST
    state = jnp.pad(jnp.transpose(dofs, (1, 0, 2)), ((0, 0), (0, NBP - NB), (0, 0)))
    stiff = stacked(jnp.pad(-stiffness, ((0, 0), (0, NBP - NB), (0, NBK - NB))).reshape(3 * NBP, NBK))
    proj = stacked(jnp.pad(face_proj, ((0, 0), (0, 1), (0, NBK - NB))).reshape(4 * NFP, NBK))
    far_lift = jnp.einsum("igb,ogf->biof", face_proj, face_rot, precision=high)
    far_lift = jnp.pad(far_lift, ((0, NBP - NB), (0, 0), (0, 0), (0, 1))).reshape(NBP, 12 * NFP)
    far_hi, far_lo = split(far_lift)
    lift_a, lift_b = jnp.concatenate([far_hi, far_lo], axis=0), far_hi
    own_lift = jnp.pad(jnp.transpose(face_proj, (2, 0, 1)), ((0, NBP - NB), (0, 0), (0, 1)))
    own_lift = stacked(own_lift.reshape(NBP, 4 * NFP))

    codes = neighbour.reshape(1, FACES)
    near = (jnp.arange(FACES, dtype=jnp.int32)[:, None] == codes).astype(BF)
    slot = jnp.bitwise_xor((codes - FACES) // 4, sub * H)
    slot = jnp.where((codes >= FACES) & (codes < FACES + 4 * SLOTS), slot, -1)
    row = jnp.arange(SLOTS, dtype=jnp.int32)
    arrived_slot = (row // H % 3) * 32 + row // 24 * H + row % H
    far = (arrived_slot[:, None] == slot).astype(BF)
    listed = send_list.reshape(3, 4, H)
    order = jnp.bitwise_xor(jnp.arange(4, dtype=jnp.int32), sub)
    listed = jnp.take(listed, order, axis=1).reshape(SLOTS, 1)
    pick = (listed == jnp.arange(FACES, dtype=jnp.int32)[None, :]).astype(BF)
    omask = (orient[:, None, :] == jnp.arange(3, dtype=jnp.int32)[None, :, None]).astype(BF)
    omask = jnp.broadcast_to(omask.reshape(12, 1, E), (12, NFP, E))

    period = jnp.left_shift(jnp.int32(1), cluster)
    scale = period.astype(F32)
    masks, weights = [], []
    for step in range(STEPS):
        offset = step % period
        masks.append((offset == 0).astype(F32))
        a = offset.astype(F32)
        low, high_ = jnp.ones_like(a), jnp.ones_like(a)
        div = jnp.ones_like(a)
        for k in range(ORDER):
            low, high_ = low * a, high_ * (a + 1.0)
            weights.append((high_ - low) / (div * FACT[k + 1]))
            div = div * scale
    masks, weights = jnp.stack(masks), jnp.stack(weights)
    period_rows = jnp.broadcast_to(scale[None, :], (8, E))

    n_dom, n_sub = lax.axis_size("dom"), lax.axis_size("sub")
    down = [(i, (i - 1) % n_dom) for i in range(n_dom)]
    up = [(i, (i + 1) % n_dom) for i in range(n_dom)]

    terms_s = ((ORDER, NV, NBP, E), F32)
    face_s = ((WIDE, FACES), BF)
    pay_s = ((32, WIDE), F32)
    nsum_s = ((WIDE, FACES), F32)
    base_s = ((NV, NBP, E), F32)
    xs_s = ((3 * NBK, COLS), BF)
    xg_s = ((384, COLS), BF)
    xq_s = ((192, COLS), BF)
    sends = [terms_s, face_s, face_s, pay_s, pay_s, pay_s]
    for step in range(STEPS):
        tail = [stiff, star, proj, weights, pick]
        if step == 0:
            terms, d_hi, d_lo, p_lo, p_own, p_hi = call(
                functools.partial(critical, True, False, 0), sends, [xs_s], [state] + tail
            )
        else:
            nsum, terms, d_hi, d_lo, p_lo, p_own, p_hi = call(
                functools.partial(critical, False, False, step),
                [nsum_s] + sends,
                [xg_s, xs_s],
                came + [nsum, base, neighbour_flux, lift_a, lift_b, omask, far] + tail + [masks, terms],
            )
        r_lo = lax.ppermute(p_lo, "dom", down)
        r_hi = lax.ppermute(p_hi, "dom", up)
        common = [terms, d_hi, d_lo, near, stiff, star, proj, local_flux, own_lift, period_rows]
        if step == 0:
            nsum, base = call(functools.partial(beside, True, 0), [nsum_s, base_s], [xs_s, xq_s], common)
        else:
            nsum, base = call(
                functools.partial(beside, False, step), [nsum_s, base_s], [xs_s, xq_s], common + [masks, nsum, base]
            )
        came = [r_lo, r_hi]
        for r in range(1, 4):
            rows = slice(r * H, (r + 1) * H)
            block = jnp.concatenate([r_lo[rows], p_own[rows], r_hi[rows]], axis=0)
            came.append(lax.ppermute(block, "sub", [(i, i ^ r) for i in range(n_sub)]))
    (out,) = call(
        functools.partial(critical, False, True, STEPS),
        [((NV, NB, E), F32)],
        [xg_s],
        came + [nsum, base, neighbour_flux, lift_a, lift_b, omask, far],
    )
    return jnp.transpose(out, (1, 0, 2))


def solution(mesh):
    placed = (
        P(None, None, ("dom", "sub")),
        P(),
        P(None, None, None, ("dom", "sub")),
        P(None, None, None, ("dom", "sub")),
        P(None, None, None, ("dom", "sub")),
        P(),
        P(),
        P(("dom", "sub")),
        P(None, ("dom", "sub")),
        P(None, ("dom", "sub")),
        P("dom", "sub", None),
    )
    return jax.shard_map(
        body, mesh=mesh, in_specs=placed, out_specs=P(None, None, ("dom", "sub")), check_vma=False
    )
```

```python
import functools

import jax
import jax.numpy as jnp
from jax import lax
from jax.experimental import pallas as pl
from jax.experimental.pallas import tpu as pltpu
from jax.sharding import PartitionSpec as P

ORDER = 5
STEPS = 8
NB = 35
NBP = 40
NBK = 48
NF = 15
NFP = 16
NV = 9
E = 128
H = 8
SLOTS = 96
FACES = 4 * E
WIDE = NV * NFP
COLS = NV * E
FACT = [1.0, 1.0, 2.0, 6.0, 24.0, 120.0, 720.0]
BF = jnp.bfloat16
F32 = jnp.float32


def halves(x):
    hi = x.astype(BF)
    lo = (x - hi.astype(F32)).astype(BF)
    return hi, lo


def dot(a, b):
    return jnp.dot(a, b, preferred_element_type=F32)


def fill_basis(xs_ref, values):
    pad = jnp.zeros((NBK - NBP, E), F32)
    for v in range(NV):
        hi, lo = halves(jnp.concatenate([values[v], pad], axis=0))
        cols = slice(v * E, (v + 1) * E)
        xs_ref[0:NBK, cols] = hi
        xs_ref[NBK : 2 * NBK, cols] = lo
        xs_ref[2 * NBK : 3 * NBK, cols] = hi


def derive(values, stiff_ref, star_ref, xs_ref):
    fill_basis(xs_ref, values)
    applied = dot(stiff_ref[...], xs_ref[...])
    acc = [None] * NV
    for d in range(3):
        for u in range(NV):
            part = applied[d * NBP : (d + 1) * NBP, u * E : (u + 1) * E]
            for v in range(NV):
                term = part * star_ref[u, v, d : d + 1, :]
                acc[v] = term if acc[v] is None else acc[v] + term
    return acc


def weight_rows(cluster_ref, step):
    period = jnp.left_shift(jnp.int32(1), cluster_ref[...])
    offset = jnp.bitwise_and(jnp.int32(step), period - 1)
    a, inverse = offset.astype(F32), 1.0 / period.astype(F32)
    low, high, scale, rows = jnp.ones_like(a), jnp.ones_like(a), jnp.ones_like(a), []
    for k in range(ORDER):
        low, high = low * a, high * (a + 1.0)
        rows.append((high - low) * scale * (1.0 / FACT[k + 1]))
        scale = scale * inverse
    return rows, offset == 0


def expand(step, first, upd, cluster, stiff, star, proj, pick, terms_in, terms, d_hi, d_lo, pay_swap, pay_rest, xs):
    rows, start = weight_rows(cluster, step)
    current = upd
    total = [None] * NV
    for k in range(ORDER):
        if k > 0:
            current = derive(current, stiff, star, xs)
        for v in range(NV):
            kept = current[v] if first else jnp.where(start, current[v], terms_in[k, v])
            terms[k, v] = kept
            part = kept * rows[k]
            total[v] = part if k == 0 else total[v] + part
    fill_basis(xs, total)
    faces = dot(proj[...], xs[...])
    for i in range(4):
        for v in range(NV):
            hi, lo = halves(faces[i * NFP : (i + 1) * NFP, v * E : (v + 1) * E])
            d_hi[v * NFP : (v + 1) * NFP, i * E : (i + 1) * E] = hi
            d_lo[v * NFP : (v + 1) * NFP, i * E : (i + 1) * E] = lo
    dims = (((1,), (1,)), ((), ()))
    pay = lax.dot_general(pick[...], d_hi[...], dims, preferred_element_type=F32)
    pay = pay + lax.dot_general(pick[...], d_lo[...], dims, preferred_element_type=F32)
    pay_swap[...] = pay[0:32]
    pay_rest[...] = pay[32:160]


def opening(*refs):
    raw, refs = refs[:11], list(refs[11:])
    take = lambda n: [refs.pop(0) for _ in range(n)]
    odd_ref = refs.pop(0)
    neighbour_ref, cluster, orient = take(3)
    stiff, proj, star, nflux, lflux, lift_a, lift_b, own_lift, far, pick = take(10)
    terms, d_hi, d_lo, pay_swap, pay_rest = take(5)
    dofs_s, stiff_s, proj_s, rot_s, send_ref, state, wide_s, tall_s, xs, sems = take(10)
    targets = [send_ref, neighbour_ref, stiff_s, proj_s, rot_s, cluster, dofs_s, star, nflux, lflux, orient]
    copies = [pltpu.make_async_copy(raw[n], targets[n], sems.at[n]) for n in range(11)]
    for copy in copies:
        copy.start()
    for copy in copies[:2]:
        copy.wait()

    high = lax.Precision.HIGHEST
    columns_first = (((0,), (0,)), ((), ()))

    def grid(shape):
        return lax.broadcasted_iota(jnp.int32, shape, 0), lax.broadcasted_iota(jnp.int32, shape, 1)

    odd = odd_ref[...]
    codes = neighbour_ref[...]
    slot = jnp.right_shift(codes - FACES, 2)
    block, source, place = slot >> 5, jnp.bitwise_and(slot >> 3, 3), jnp.bitwise_and(slot, 7)
    same, cross = 4 * (1 - odd), 4 * odd
    row = jnp.where(block == 2 * (1 - odd), (cross + source) * 16 + place, (same + source) * 16 + place)
    row = jnp.where(block == 2 * odd, row + H, row)
    row = jnp.where((codes >= FACES) & (codes < FACES + 4 * SLOTS), row, -1)
    rows, _ = grid((128, E))
    for i in range(4):
        far[:, i * E : (i + 1) * E] = (rows == row[i : i + 1, :]).astype(F32).astype(BF)
    rows, columns = grid((160, SLOTS))
    flag = odd[:, 0:1]
    rest = rows - 32
    peer, place = rest >> 4, jnp.bitwise_and(rest, 15)
    inside = jnp.where((peer >> 2) == 1 - flag, 32, 64 * flag)
    wanted = inside + jnp.bitwise_and(peer, 3) * H + place
    wanted = jnp.where(rest < 0, 64 * (1 - flag) + rows, jnp.where(place < H, wanted, -1))
    chooser = (columns == wanted).astype(F32)
    listed = jnp.broadcast_to(send_ref[...].astype(F32), (8, SLOTS))
    listed = lax.dot_general(chooser, listed, (((1,), (1,)), ((), ())), precision=high, preferred_element_type=F32)
    listed = jnp.where(wanted[:, 0:1] < 0, float(FACES), listed[:, 0:1])
    _, columns = grid((160, FACES))
    pick[...] = (columns.astype(F32) == listed).astype(F32).astype(BF)

    for copy in copies[2:5]:
        copy.wait()
    wide_s[...] = jnp.zeros_like(wide_s)
    for d in range(3):
        wide_s[d * NBP : d * NBP + NB, 0:NB] = -stiff_s[d]
    rows, columns = grid((NBK, 3 * NBK))
    twice = ((columns == rows) | (columns == rows + NBK)).astype(F32).astype(BF)
    once = (columns == rows + 2 * NBK).astype(F32).astype(BF)
    hi, lo = halves(wide_s[...])
    stiff[...] = (dot(hi, twice) + dot(lo, once)).astype(BF)
    tall_s[...] = jnp.zeros_like(tall_s)
    for i in range(4):
        for f in range(NF):
            tall_s[i * NFP + f : i * NFP + f + 1, 0:NB] = proj_s[f, i : i + 1, :]
    hi, lo = halves(tall_s[...])
    proj[...] = (dot(hi, twice) + dot(lo, once)).astype(BF)
    rows, columns = grid((64, 192))
    twice = ((columns == rows) | (columns == rows + 64)).astype(F32).astype(BF)
    once = (columns == rows + 128).astype(F32).astype(BF)
    own = lax.dot_general(hi, twice, columns_first, preferred_element_type=F32)
    own = own + lax.dot_general(lo, once, columns_first, preferred_element_type=F32)
    own_lift[...] = own[0:NBP].astype(BF)
    mixed = jnp.zeros((64, 192), F32)
    to_rows, to_columns = grid((64, NF))
    from_rows, from_columns = grid((NF, 192))
    for o in range(3):
        spread = (jnp.bitwise_and(to_rows, 15) == to_columns).astype(F32)
        spread = jnp.dot(spread, rot_s[o], precision=high, preferred_element_type=F32)
        group = from_columns // 48
        placed = (from_columns - 48 * group == o * NFP + from_rows).astype(F32)
        mixed = mixed + jnp.dot(spread, placed, precision=high, preferred_element_type=F32)
    mixed = jnp.where((rows >> 4) == columns // 48, mixed, 0.0)
    lift = lax.dot_general(tall_s[...], mixed, columns_first, precision=high, preferred_element_type=F32)
    hi, lo = halves(lift[0:NBP])
    lift_a[0:NBP, :] = hi
    lift_a[NBP : 2 * NBP, :] = lo
    lift_b[...] = hi

    for copy in copies[5:]:
        copy.wait()
    state[...] = jnp.zeros_like(state)
    for v in range(NV):
        state[v, 0:NB, :] = dofs_s[v]
    upd = [state[v] for v in range(NV)]
    expand(0, True, upd, cluster, stiff, star, proj, pick, None, terms, d_hi, d_lo, pay_swap, pay_rest, xs)


def critical(last, step, *refs):
    refs = list(refs)
    take = lambda n: [refs.pop(0) for _ in range(n)]
    got_ref, nsum_ref, base_ref, nflux, lift_a, lift_b, orient, far = take(8)
    if last:
        out_ref, xg = take(2)
    else:
        stiff, star, proj, pick, cluster, terms_in = take(6)
        nsum_out, terms, d_hi, d_lo, pay_swap, pay_rest, xg, xs = take(8)

    got_hi, got_lo = halves(got_ref[...])
    dims = (((0,), (0,)), ((), ()))
    arrived = lax.dot_general(got_hi, far[...], dims, preferred_element_type=F32)
    arrived = arrived + lax.dot_general(got_lo, far[...], dims, preferred_element_type=F32)
    total = nsum_ref[...] + arrived
    if not last:
        nsum_out[...] = total
    for i in range(4):
        acc = [None] * NV
        for u in range(NV):
            part = total[u * NFP : (u + 1) * NFP, i * E : (i + 1) * E]
            for v in range(NV):
                term = part * nflux[u, v, i : i + 1, :]
                acc[v] = term if acc[v] is None else acc[v] + term
        chosen = []
        for o in range(3):
            mask = (orient[i : i + 1, :] == o).astype(F32)
            chosen.append(jnp.broadcast_to(mask, (NFP, E)).astype(BF))
        for v in range(NV):
            hi, lo = halves(acc[v])
            for o in range(3):
                row = (i * 3 + o) * NFP
                cols = slice(v * E, (v + 1) * E)
                xg[row : row + NFP, cols] = hi * chosen[o]
                xg[192 + row : 192 + row + NFP, cols] = lo * chosen[o]
    two = dot(lift_a[...], xg[0:192, :])
    lifted = two[0:NBP] + two[NBP : 2 * NBP] + dot(lift_b[...], xg[192:384, :])
    upd = [base_ref[v] + lifted[:, v * E : (v + 1) * E] for v in range(NV)]
    if last:
        for v in range(NV):
            out_ref[v] = upd[v][0:NB]
    else:
        expand(step, False, upd, cluster, stiff, star, proj, pick, terms_in, terms, d_hi, d_lo, pay_swap, pay_rest, xs)


def beside(first, step, *refs):
    refs = list(refs)
    take = lambda n: [refs.pop(0) for _ in range(n)]
    terms, d_hi, d_lo, neighbour, stiff, star, proj, lflux, own_lift, cluster = take(10)
    if not first:
        nsum_ref, base_ref = take(2)
    nsum_out, base_out, xs, xq = take(4)
    _, start = weight_rows(cluster, step)
    period = jnp.left_shift(jnp.int32(1), cluster[...]).astype(F32)
    face_rows = lax.broadcasted_iota(jnp.int32, (FACES, E), 0)
    for i in range(4):
        cols = slice(i * E, (i + 1) * E)
        near = (face_rows == neighbour[i : i + 1, :]).astype(F32).astype(BF)
        gathered = dot(d_hi[...], near) + dot(d_lo[...], near)
        nsum_out[:, cols] = gathered if first else gathered + jnp.where(start, 0.0, nsum_ref[:, cols])
    final = derive([terms[ORDER - 1, v] for v in range(NV)], stiff, star, xs)
    state = []
    whole = []
    for v in range(NV):
        volume = final[v] * (1.0 / FACT[ORDER])
        own = terms[0, v]
        for k in range(1, ORDER):
            volume = volume + terms[k, v] * (1.0 / FACT[k])
            own = own + terms[k, v] * (1.0 / FACT[k + 1])
        state.append(terms[0, v] + volume)
        whole.append(own * period)
    fill_basis(xs, whole)
    faces = dot(proj[...], xs[...])
    for i in range(4):
        acc = [None] * NV
        for u in range(NV):
            part = faces[i * NFP : (i + 1) * NFP, u * E : (u + 1) * E]
            for v in range(NV):
                term = part * lflux[u, v, i : i + 1, :]
                acc[v] = term if acc[v] is None else acc[v] + term
        for v in range(NV):
            hi, lo = halves(acc[v])
            cols = slice(v * E, (v + 1) * E)
            xq[i * NFP : (i + 1) * NFP, cols] = hi
            xq[64 + i * NFP : 64 + (i + 1) * NFP, cols] = lo
            xq[128 + i * NFP : 128 + (i + 1) * NFP, cols] = hi
    lifted = dot(own_lift[...], xq[...])
    for v in range(NV):
        fresh = state[v] - lifted[:, v * E : (v + 1) * E]
        base_out[v] = fresh if first else jnp.where(start, fresh, base_ref[v])


def call(kernel, outs, scratch, args, raw=0):
    def memory(s):
        return pltpu.VMEM(*s) if isinstance(s, tuple) else s

    return pl.pallas_call(
        kernel,
        out_shape=[jax.ShapeDtypeStruct(s, t) for s, t in outs],
        in_specs=[pl.BlockSpec(memory_space=pltpu.HBM if n < raw else pltpu.VMEM) for n in range(len(args))],
        out_specs=[pl.BlockSpec(memory_space=pltpu.VMEM)] * len(outs),
        scratch_shapes=[memory(s) for s in scratch],
        compiler_params=pltpu.CompilerParams(vmem_limit_bytes=40 * 1024 * 1024),
    )(*args)


def body(dofs, stiffness, star, local_flux, neighbour_flux, face_proj, face_rot, cluster, neighbour, orient, send_list):
    n_dom, n_sub = lax.axis_size("dom"), lax.axis_size("sub")
    odd = lax.axis_index("dom") % 2
    chip = [(i, i ^ 1) for i in range(n_dom)]
    groups = [
        [(i + h) % n_dom * n_sub + t for h in range(2) for t in range(n_sub)] for i in range(1, n_dom, 2)
    ]
    holds_swapped = (jnp.arange(8, dtype=jnp.int32) // 4 == 1 - odd)[:, None, None]
    raw = [
        send_list.reshape(1, SLOTS),
        neighbour,
        stiffness,
        jnp.transpose(face_proj, (1, 0, 2)),
        face_rot,
        cluster.reshape(1, E),
        jnp.transpose(dofs, (1, 0, 2)),
        jnp.transpose(star, (1, 2, 0, 3)),
        jnp.transpose(neighbour_flux, (1, 2, 0, 3)),
        jnp.transpose(local_flux, (1, 2, 0, 3)),
        orient,
    ]
    raw = [pltpu.with_memory_space_constraint(x, pltpu.HBM) for x in raw]
    flux_s = ((NV, NV, 4, E), F32)
    constants = [
        ((4, E), jnp.int32),
        ((1, E), jnp.int32),
        ((4, E), jnp.int32),
        ((3 * NBP, 3 * NBK), BF),
        ((4 * NFP, 3 * NBK), BF),
        ((NV, NV, 3, E), F32),
        flux_s,
        flux_s,
        ((2 * NBP, 192), BF),
        ((NBP, 192), BF),
        ((NBP, 192), BF),
        ((128, FACES), BF),
        ((160, FACES), BF),
    ]
    terms_s = ((ORDER, NV, NBP, E), F32)
    face_s = ((WIDE, FACES), BF)
    nsum_s = ((WIDE, FACES), F32)
    base_s = ((NV, NBP, E), F32)
    xs_s = ((3 * NBK, COLS), BF)
    xg_s = ((384, COLS), BF)
    xq_s = ((192, COLS), BF)
    sends = [terms_s, face_s, face_s, ((32, WIDE), F32), ((128, WIDE), F32)]
    fetched = [
        ((NV, NB, E), F32),
        ((3, NB, NB), F32),
        ((NF, 4, NB), F32),
        ((3, NF, NF), F32),
        ((1, SLOTS), jnp.int32),
        base_s,
        ((3 * NBP, NBK), F32),
        ((4 * NFP, NBK), F32),
        xs_s,
        pltpu.SemaphoreType.DMA((11,)),
    ]
    begun = call(
        opening,
        constants + sends,
        fetched,
        raw + [jnp.full((1, E), odd, jnp.int32)],
        raw=11,
    )
    neighbour, cluster, orient = begun[:3]
    stiff, proj, star, nflux, lflux, lift_a, lift_b, own_lift, far, pick = begun[3:13]
    terms, d_hi, d_lo, p_swap, p_rest = begun[13:]
    for step in range(STEPS):
        if step > 0:
            nsum, terms, d_hi, d_lo, p_swap, p_rest = call(
                functools.partial(critical, False, step),
                [nsum_s] + sends,
                [xg_s, xs_s],
                [came, nsum, base, nflux, lift_a, lift_b, orient, far, stiff, star, proj, pick, cluster, terms],
            )
        swapped = lax.ppermute(p_swap, "dom", chip)
        old = [] if step == 0 else [nsum, base]
        nsum, base = call(
            functools.partial(beside, step == 0, step),
            [nsum_s, base_s],
            [xs_s, xq_s],
            [terms, d_hi, d_lo, neighbour, stiff, star, proj, lflux, own_lift, cluster] + old,
        )
        swapped = swapped.reshape(4, H, WIDE)
        swapped = jnp.where(holds_swapped, jnp.concatenate([swapped, swapped]), 0.0)
        p_rest = p_rest.reshape(8, 16, WIDE)
        block = jnp.concatenate([p_rest[:, 0:H], swapped], axis=1)
        block, nsum, base = lax.optimization_barrier((block, nsum, base))
        came = lax.all_to_all(
            block, ("dom", "sub"), split_axis=0, concat_axis=0, tiled=True, axis_index_groups=groups
        ).reshape(128, WIDE)
    (out,) = call(
        functools.partial(critical, True, STEPS),
        [((NV, NB, E), F32)],
        [xg_s],
        [came, nsum, base, nflux, lift_a, lift_b, orient, far],
    )
    return jnp.transpose(out, (1, 0, 2))


def solution(mesh):
    placed = (
        P(None, None, ("dom", "sub")),
        P(),
        P(None, None, None, ("dom", "sub")),
        P(None, None, None, ("dom", "sub")),
        P(None, None, None, ("dom", "sub")),
        P(),
        P(),
        P(("dom", "sub")),
        P(None, ("dom", "sub")),
        P(None, ("dom", "sub")),
        P("dom", "sub", None),
    )
    return jax.shard_map(
        body, mesh=mesh, in_specs=placed, out_specs=P(None, None, ("dom", "sub")), check_vma=False
    )
```

```python
import functools

import jax
import jax.numpy as jnp
from jax import lax
from jax.experimental import pallas as pl
from jax.experimental.pallas import tpu as pltpu
from jax.sharding import PartitionSpec as P

ORDER = 5
STEPS = 8
NB = 35
NBP = 40
NBK = 48
NF = 15
NFP = 16
NV = 9
E = 128
H = 8
SLOTS = 96
FACES = 4 * E
WIDE = NV * NFP
COLS = NV * E
FACT = [1.0, 1.0, 2.0, 6.0, 24.0, 120.0, 720.0]
BF = jnp.bfloat16
F32 = jnp.float32


def halves(x):
    hi = x.astype(BF)
    lo = (x - hi.astype(F32)).astype(BF)
    return hi, lo


def dot(a, b):
    return jnp.dot(a, b, preferred_element_type=F32)


def fill_basis(xs_ref, values):
    pad = jnp.zeros((NBK - NBP, E), F32)
    for v in range(len(values)):
        hi, lo = halves(jnp.concatenate([values[v], pad], axis=0))
        cols = slice(v * E, (v + 1) * E)
        xs_ref[0:NBK, cols] = hi
        xs_ref[NBK : 2 * NBK, cols] = lo
        xs_ref[2 * NBK : 3 * NBK, cols] = hi


def derive(values, stiff_ref, star_ref, xs_ref):
    fill_basis(xs_ref, values)
    stiff = stiff_ref[...]
    chunks = [range(0, 4), range(4, 8), range(8, 9)]
    applied = [dot(stiff, xs_ref[:, c[0] * E : (c[-1] + 1) * E]) for c in chunks]
    acc = [None] * NV
    for chunk, piece in zip(chunks, applied):
        for d in range(3):
            for n, u in enumerate(chunk):
                part = piece[d * NBP : (d + 1) * NBP, n * E : (n + 1) * E]
                for v in range(NV):
                    term = part * star_ref[u, v, d : d + 1, :]
                    acc[v] = term if acc[v] is None else acc[v] + term
    return acc


def lane_group(shape):
    return lax.broadcasted_iota(jnp.int32, shape, len(shape) - 1) >> 5


def shifted(x, groups):
    return x if groups % 4 == 0 else pltpu.roll(x, groups % 4 * 32, x.ndim - 1)


def side_by_side(values):
    group = lane_group(values[0].shape)
    parts = []
    for j in range(3):
        part = jnp.zeros_like(values[0])
        for g in range(min(4, len(values) - 4 * j)):
            part = jnp.where(group == g, shifted(values[4 * j + g], g), part)
        parts.append(part)
    return parts


def apart(parts):
    return [shifted(parts[v // 4], -(v % 4)) for v in range(NV)]


def thin_matrices(full_ref, thin_ref):
    picks = []
    for to in range(2):
        for of in range(2):
            for r in range(4):
                picks.append([(4 * of + (g - r) % 4, 4 * to + g) for g in range(4)])
    picks += [[(8, g) for g in range(4)], [(8, 4 + g) for g in range(4)]]
    picks += [[(g, 8) for g in range(4)], [(4 + g, 8) for g in range(4)], [(8, 8)]]
    depth = full_ref.shape[2]
    group = lane_group((depth, E))
    for n, sources in enumerate(picks):
        row = jnp.zeros((depth, E), F32)
        for g, (u, v) in enumerate(sources):
            row = jnp.where(group == g, shifted(full_ref[u, v], g), row)
        thin_ref[n] = row


def mix(acc, parts, thin_ref, d):
    first, second, third = parts
    spread = third + shifted(third, 1)
    spread = spread + shifted(spread, 2)
    terms = [[], [], []]
    for r in range(4):
        one, two = shifted(first, r), shifted(second, r)
        for to in range(2):
            terms[to].append(one * thin_ref[8 * to + r, d : d + 1, :])
            terms[to].append(two * thin_ref[8 * to + 4 + r, d : d + 1, :])
    for to in range(2):
        terms[to].append(spread * thin_ref[16 + to, d : d + 1, :])
    terms[2] = [part * thin_ref[18 + n, d : d + 1, :] for n, part in enumerate(parts)]
    for to in range(3):
        for term in terms[to]:
            acc[to] = term if acc[to] is None else acc[to] + term


def mixed_parts(acc):
    last = acc[2] + shifted(acc[2], 2)
    last = last + shifted(last, 1)
    return [acc[0], acc[1], jnp.where(lane_group(last.shape) == 0, last, 0.0)]


def derive_thin(parts, stiff_ref, thin_ref, xt_ref):
    fill_basis(xt_ref, parts)
    applied = dot(stiff_ref[...], xt_ref[...])
    acc = [None] * 3
    for d in range(3):
        rows = applied[d * NBP : (d + 1) * NBP]
        mix(acc, [rows[:, j * E : (j + 1) * E] for j in range(3)], thin_ref, d)
    return mixed_parts(acc)


def weight_rows(cluster_ref, step):
    period = jnp.left_shift(jnp.int32(1), cluster_ref[...])
    offset = jnp.bitwise_and(jnp.int32(step), period - 1)
    a, inverse = offset.astype(F32), 1.0 / period.astype(F32)
    low, high, scale, rows = jnp.ones_like(a), jnp.ones_like(a), jnp.ones_like(a), []
    for k in range(ORDER):
        low, high = low * a, high * (a + 1.0)
        rows.append((high - low) * scale * (1.0 / FACT[k + 1]))
        scale = scale * inverse
    return rows, offset == 0


def expand_thin(step, upd, cluster, stiff, thin, proj, pick, terms_in, terms, d_hi, d_lo, pay_swap, pay_rest, xs, xt):
    rows, start = weight_rows(cluster, step)
    current = side_by_side(upd)
    fresh = [None] * 3
    for k in range(ORDER):
        if k > 0:
            current = derive_thin(current, stiff, thin, xt)
        for j in range(3):
            terms[k, j] = current[j]
            part = current[j] * (1.0 / FACT[k + 1])
            fresh[j] = part if k == 0 else fresh[j] + part
    fresh = apart(fresh)
    total = []
    for v in range(NV):
        kept = terms_in[0, v] * rows[0]
        for k in range(1, ORDER):
            kept = kept + terms_in[k, v] * rows[k]
        total.append(jnp.where(start, fresh[v], kept))
    send(total, proj, pick, d_hi, d_lo, pay_swap, pay_rest, xs)


def expand(step, first, upd, cluster, stiff, star, proj, pick, terms_in, terms, d_hi, d_lo, pay_swap, pay_rest, xs):
    rows, start = weight_rows(cluster, step)
    current = upd
    total = [None] * NV
    for k in range(ORDER):
        if k > 0:
            current = derive(current, stiff, star, xs)
        for v in range(NV):
            kept = current[v] if first else jnp.where(start, current[v], terms_in[k, v])
            terms[k, v] = kept
            part = kept * rows[k]
            total[v] = part if k == 0 else total[v] + part
    send(total, proj, pick, d_hi, d_lo, pay_swap, pay_rest, xs)


def send(total, proj, pick, d_hi, d_lo, pay_swap, pay_rest, xs):
    fill_basis(xs, total)
    faces = dot(proj[...], xs[...])
    for i in range(4):
        for v in range(NV):
            hi, lo = halves(faces[i * NFP : (i + 1) * NFP, v * E : (v + 1) * E])
            d_hi[v * NFP : (v + 1) * NFP, i * E : (i + 1) * E] = hi
            d_lo[v * NFP : (v + 1) * NFP, i * E : (i + 1) * E] = lo
    dims = (((1,), (1,)), ((), ()))
    pay = lax.dot_general(pick[...], d_hi[...], dims, preferred_element_type=F32)
    pay = pay + lax.dot_general(pick[...], d_lo[...], dims, preferred_element_type=F32)
    pay_swap[...] = pay[0:32]
    pay_rest[...] = pay[32:160]


def opening(*refs):
    raw, refs = refs[:11], list(refs[11:])
    take = lambda n: [refs.pop(0) for _ in range(n)]
    odd_ref = refs.pop(0)
    neighbour_ref, cluster, orient = take(3)
    stiff, proj, star, nflux, lflux, lift_a, lift_b, own_lift, far, pick = take(10)
    terms, d_hi, d_lo, pay_swap, pay_rest = take(5)
    dofs_s, stiff_s, proj_s, rot_s, send_ref, state, wide_s, tall_s, xs, sems = take(10)
    targets = [send_ref, neighbour_ref, stiff_s, proj_s, rot_s, cluster, dofs_s, star, nflux, lflux, orient]
    copies = [pltpu.make_async_copy(raw[n], targets[n], sems.at[n]) for n in range(11)]
    for copy in copies:
        copy.start()
    for copy in copies[:2]:
        copy.wait()

    high = lax.Precision.HIGHEST
    columns_first = (((0,), (0,)), ((), ()))

    def grid(shape):
        return lax.broadcasted_iota(jnp.int32, shape, 0), lax.broadcasted_iota(jnp.int32, shape, 1)

    odd = odd_ref[...]
    codes = neighbour_ref[...]
    slot = jnp.right_shift(codes - FACES, 2)
    block, source, place = slot >> 5, jnp.bitwise_and(slot >> 3, 3), jnp.bitwise_and(slot, 7)
    same, cross = 4 * (1 - odd), 4 * odd
    row = jnp.where(block == 2 * (1 - odd), (cross + source) * 16 + place, (same + source) * 16 + place)
    row = jnp.where(block == 2 * odd, row + H, row)
    row = jnp.where((codes >= FACES) & (codes < FACES + 4 * SLOTS), row, -1)
    rows, _ = grid((128, E))
    for i in range(4):
        far[:, i * E : (i + 1) * E] = (rows == row[i : i + 1, :]).astype(F32).astype(BF)
    rows, columns = grid((160, SLOTS))
    flag = odd[:, 0:1]
    rest = rows - 32
    peer, place = rest >> 4, jnp.bitwise_and(rest, 15)
    inside = jnp.where((peer >> 2) == 1 - flag, 32, 64 * flag)
    wanted = inside + jnp.bitwise_and(peer, 3) * H + place
    wanted = jnp.where(rest < 0, 64 * (1 - flag) + rows, jnp.where(place < H, wanted, -1))
    chooser = (columns == wanted).astype(F32)
    listed = jnp.broadcast_to(send_ref[...].astype(F32), (8, SLOTS))
    listed = lax.dot_general(chooser, listed, (((1,), (1,)), ((), ())), precision=high, preferred_element_type=F32)
    listed = jnp.where(wanted[:, 0:1] < 0, float(FACES), listed[:, 0:1])
    _, columns = grid((160, FACES))
    pick[...] = (columns.astype(F32) == listed).astype(F32).astype(BF)

    for copy in copies[2:5]:
        copy.wait()
    wide_s[...] = jnp.zeros_like(wide_s)
    for d in range(3):
        wide_s[d * NBP : d * NBP + NB, 0:NB] = -stiff_s[d]
    rows, columns = grid((NBK, 3 * NBK))
    twice = ((columns == rows) | (columns == rows + NBK)).astype(F32).astype(BF)
    once = (columns == rows + 2 * NBK).astype(F32).astype(BF)
    hi, lo = halves(wide_s[...])
    stiff[...] = (dot(hi, twice) + dot(lo, once)).astype(BF)
    tall_s[...] = jnp.zeros_like(tall_s)
    for i in range(4):
        for f in range(NF):
            tall_s[i * NFP + f : i * NFP + f + 1, 0:NB] = proj_s[f, i : i + 1, :]
    hi, lo = halves(tall_s[...])
    proj[...] = (dot(hi, twice) + dot(lo, once)).astype(BF)
    rows, columns = grid((64, 192))
    twice = ((columns == rows) | (columns == rows + 64)).astype(F32).astype(BF)
    once = (columns == rows + 128).astype(F32).astype(BF)
    own = lax.dot_general(hi, twice, columns_first, preferred_element_type=F32)
    own = own + lax.dot_general(lo, once, columns_first, preferred_element_type=F32)
    own_lift[...] = own[0:NBP].astype(BF)
    mixed = jnp.zeros((64, 192), F32)
    to_rows, to_columns = grid((64, NF))
    from_rows, from_columns = grid((NF, 192))
    for o in range(3):
        spread = (jnp.bitwise_and(to_rows, 15) == to_columns).astype(F32)
        spread = jnp.dot(spread, rot_s[o], precision=high, preferred_element_type=F32)
        group = from_columns // 48
        placed = (from_columns - 48 * group == o * NFP + from_rows).astype(F32)
        mixed = mixed + jnp.dot(spread, placed, precision=high, preferred_element_type=F32)
    mixed = jnp.where((rows >> 4) == columns // 48, mixed, 0.0)
    lift = lax.dot_general(tall_s[...], mixed, columns_first, precision=high, preferred_element_type=F32)
    hi, lo = halves(lift[0:NBP])
    lift_a[0:NBP, :] = hi
    lift_a[NBP : 2 * NBP, :] = lo
    lift_b[...] = hi

    for copy in copies[5:]:
        copy.wait()
    state[...] = jnp.zeros_like(state)
    for v in range(NV):
        state[v, 0:NB, :] = dofs_s[v]
    upd = [state[v] for v in range(NV)]
    expand(0, True, upd, cluster, stiff, star, proj, pick, None, terms, d_hi, d_lo, pay_swap, pay_rest, xs)


def critical(last, step, *refs):
    refs = list(refs)
    take = lambda n: [refs.pop(0) for _ in range(n)]
    got_ref, nsum_ref, base_ref, nflux, lift_a, lift_b, orient, far = take(8)
    if last:
        out_ref, xg = take(2)
    else:
        stiff, star, proj, pick, cluster, terms_in = take(6)
        nsum_out, terms, d_hi, d_lo, pay_swap, pay_rest, xg, xs = take(8)
        if step % 2:
            (xt,) = take(1)

    got_hi, got_lo = halves(got_ref[...])
    dims = (((0,), (0,)), ((), ()))
    arrived = lax.dot_general(got_hi, far[...], dims, preferred_element_type=F32)
    arrived = arrived + lax.dot_general(got_lo, far[...], dims, preferred_element_type=F32)
    total = nsum_ref[...] + arrived
    if not last:
        nsum_out[...] = total
    for i in range(4):
        acc = [None] * NV
        for u in range(NV):
            part = total[u * NFP : (u + 1) * NFP, i * E : (i + 1) * E]
            for v in range(NV):
                term = part * nflux[u, v, i : i + 1, :]
                acc[v] = term if acc[v] is None else acc[v] + term
        chosen = []
        for o in range(3):
            mask = (orient[i : i + 1, :] == o).astype(F32)
            chosen.append(jnp.broadcast_to(mask, (NFP, E)).astype(BF))
        for v in range(NV):
            hi, lo = halves(acc[v])
            for o in range(3):
                row = (i * 3 + o) * NFP
                cols = slice(v * E, (v + 1) * E)
                xg[row : row + NFP, cols] = hi * chosen[o]
                xg[192 + row : 192 + row + NFP, cols] = lo * chosen[o]
    two = dot(lift_a[...], xg[0:192, :])
    lifted = two[0:NBP] + two[NBP : 2 * NBP] + dot(lift_b[...], xg[192:384, :])
    upd = [base_ref[v] + lifted[:, v * E : (v + 1) * E] for v in range(NV)]
    if last:
        for v in range(NV):
            out_ref[v] = upd[v][0:NB]
    elif step % 2:
        expand_thin(
            step, upd, cluster, stiff, star, proj, pick, terms_in, terms, d_hi, d_lo, pay_swap, pay_rest, xs, xt
        )
    else:
        expand(step, False, upd, cluster, stiff, star, proj, pick, terms_in, terms, d_hi, d_lo, pay_swap, pay_rest, xs)


def beside(step, *refs):
    refs = list(refs)
    take = lambda n: [refs.pop(0) for _ in range(n)]
    first, thin = step == 0, step % 2 == 1
    terms, d_hi, d_lo, neighbour, stiff, star, proj, lflux, own_lift, cluster = take(10)
    if not first:
        nsum_ref, base_ref = take(2)
    nsum_out, base_out = take(2)
    if first:
        thin_star, thin_lflux = take(2)
    xs, xq = take(2)
    _, start = weight_rows(cluster, step)
    period = jnp.left_shift(jnp.int32(1), cluster[...]).astype(F32)
    face_rows = lax.broadcasted_iota(jnp.int32, (FACES, E), 0)
    for i in range(4):
        cols = slice(i * E, (i + 1) * E)
        near = (face_rows == neighbour[i : i + 1, :]).astype(F32).astype(BF)
        gathered = dot(d_hi[...], near) + dot(d_lo[...], near)
        nsum_out[:, cols] = gathered if first else gathered + jnp.where(start, 0.0, nsum_ref[:, cols])
    wide = 3 if thin else NV
    held = [[terms[k, v] for v in range(wide)] for k in range(ORDER)]
    if thin:
        final = derive_thin(held[ORDER - 1], stiff, star, xs)
    else:
        final = derive(held[ORDER - 1], stiff, star, xs)
    state = []
    whole = []
    for v in range(wide):
        volume = final[v] * (1.0 / FACT[ORDER])
        own = held[0][v]
        for k in range(1, ORDER):
            volume = volume + held[k][v] * (1.0 / FACT[k])
            own = own + held[k][v] * (1.0 / FACT[k + 1])
        state.append(held[0][v] + volume)
        whole.append(own if thin else own * period)
    fill_basis(xs, whole)
    faces = dot(proj[...], xs[...])
    for i in range(4):
        rows = faces[i * NFP : (i + 1) * NFP]
        acc = [None] * wide
        if thin:
            mix(acc, [rows[:, j * E : (j + 1) * E] for j in range(3)], lflux, i)
            acc = mixed_parts(acc)
        else:
            for u in range(NV):
                part = rows[:, u * E : (u + 1) * E]
                for v in range(NV):
                    term = part * lflux[u, v, i : i + 1, :]
                    acc[v] = term if acc[v] is None else acc[v] + term
        for v in range(wide):
            hi, lo = halves(acc[v])
            cols = slice(v * E, (v + 1) * E)
            xq[i * NFP : (i + 1) * NFP, cols] = hi
            xq[64 + i * NFP : 64 + (i + 1) * NFP, cols] = lo
            xq[128 + i * NFP : 128 + (i + 1) * NFP, cols] = hi
    lifted = dot(own_lift[...], xq[...])
    fresh = [state[v] - lifted[:, v * E : (v + 1) * E] for v in range(wide)]
    if thin:
        fresh = apart(fresh)
    for v in range(NV):
        base_out[v] = fresh[v] if first else jnp.where(start, fresh[v], base_ref[v])
    if first:
        thin_matrices(star, thin_star)
        thin_matrices(lflux, thin_lflux)


def call(kernel, outs, scratch, args, raw=0):
    def memory(s):
        return pltpu.VMEM(*s) if isinstance(s, tuple) else s

    return pl.pallas_call(
        kernel,
        out_shape=[jax.ShapeDtypeStruct(s, t) for s, t in outs],
        in_specs=[pl.BlockSpec(memory_space=pltpu.HBM if n < raw else pltpu.VMEM) for n in range(len(args))],
        out_specs=[pl.BlockSpec(memory_space=pltpu.VMEM)] * len(outs),
        scratch_shapes=[memory(s) for s in scratch],
        compiler_params=pltpu.CompilerParams(vmem_limit_bytes=40 * 1024 * 1024),
    )(*args)


def body(dofs, stiffness, star, local_flux, neighbour_flux, face_proj, face_rot, cluster, neighbour, orient, send_list):
    n_dom, n_sub = lax.axis_size("dom"), lax.axis_size("sub")
    odd = lax.axis_index("dom") % 2
    chip = [(i, i ^ 1) for i in range(n_dom)]
    groups = [
        [(i + h) % n_dom * n_sub + t for h in range(2) for t in range(n_sub)] for i in range(1, n_dom, 2)
    ]
    lines = [[i * n_sub + t for t in range(n_sub)] for i in range(n_dom)]
    dom = lax.axis_index("dom")
    at_end = (dom == 0) | (dom == n_dom - 1)

    def exchange(block, among):
        return lax.all_to_all(
            block, ("dom", "sub"), split_axis=0, concat_axis=0, tiled=True, axis_index_groups=among
        )

    def across_pair(block):
        return exchange(block, groups)

    def within_line(block):
        own = exchange(jnp.where(odd == 1, block[0:4], block[4:8]), lines)
        return jnp.concatenate([own, own])

    holds_swapped = (jnp.arange(8, dtype=jnp.int32) // 4 == 1 - odd)[:, None, None]
    raw = [
        send_list.reshape(1, SLOTS),
        neighbour,
        stiffness,
        jnp.transpose(face_proj, (1, 0, 2)),
        face_rot,
        cluster.reshape(1, E),
        jnp.transpose(dofs, (1, 0, 2)),
        jnp.transpose(star, (1, 2, 0, 3)),
        jnp.transpose(neighbour_flux, (1, 2, 0, 3)),
        jnp.transpose(local_flux, (1, 2, 0, 3)),
        orient,
    ]
    raw = [pltpu.with_memory_space_constraint(x, pltpu.HBM) for x in raw]
    flux_s = ((NV, NV, 4, E), F32)
    constants = [
        ((4, E), jnp.int32),
        ((1, E), jnp.int32),
        ((4, E), jnp.int32),
        ((3 * NBP, 3 * NBK), BF),
        ((4 * NFP, 3 * NBK), BF),
        ((NV, NV, 3, E), F32),
        flux_s,
        flux_s,
        ((2 * NBP, 192), BF),
        ((NBP, 192), BF),
        ((NBP, 192), BF),
        ((128, FACES), BF),
        ((160, FACES), BF),
    ]
    terms_s = ((ORDER, NV, NBP, E), F32)
    face_s = ((WIDE, FACES), BF)
    nsum_s = ((WIDE, FACES), F32)
    base_s = ((NV, NBP, E), F32)
    xs_s = ((3 * NBK, COLS), BF)
    xg_s = ((384, COLS), BF)
    xq_s = ((192, COLS), BF)
    sends = [terms_s, face_s, face_s, ((32, WIDE), F32), ((128, WIDE), F32)]
    fetched = [
        ((NV, NB, E), F32),
        ((3, NB, NB), F32),
        ((NF, 4, NB), F32),
        ((3, NF, NF), F32),
        ((1, SLOTS), jnp.int32),
        base_s,
        ((3 * NBP, NBK), F32),
        ((4 * NFP, NBK), F32),
        xs_s,
        pltpu.SemaphoreType.DMA((11,)),
    ]
    begun = call(
        opening,
        constants + sends,
        fetched,
        raw + [jnp.full((1, E), odd, jnp.int32)],
        raw=11,
    )
    neighbour, cluster, orient = begun[:3]
    stiff, proj, star, nflux, lflux, lift_a, lift_b, own_lift, far, pick = begun[3:13]
    terms, d_hi, d_lo, p_swap, p_rest = begun[13:]
    thin_s = ((ORDER, 3, NBP, E), F32)
    thin_columns = 3 * E
    for step in range(STEPS):
        odd_step = step % 2 == 1
        if odd_step:
            nsum, fresh, d_hi, d_lo, p_swap, p_rest = call(
                functools.partial(critical, False, step),
                [nsum_s, thin_s] + sends[1:],
                [xg_s, xs_s, ((3 * NBK, thin_columns), BF)],
                [came, nsum, base, nflux, lift_a, lift_b, orient, far, stiff, thin_star, proj, pick, cluster, terms],
            )
        elif step > 0:
            nsum, terms, d_hi, d_lo, p_swap, p_rest = call(
                functools.partial(critical, False, step),
                [nsum_s] + sends,
                [xg_s, xs_s],
                [came, nsum, base, nflux, lift_a, lift_b, orient, far, stiff, star, proj, pick, cluster, terms],
            )
        swapped = lax.ppermute(p_swap, "dom", chip)
        side = functools.partial(beside, step)
        if step == 0:
            nsum, base, thin_star, thin_lflux = call(
                side,
                [nsum_s, base_s, ((21, 3, E), F32), ((21, 4, E), F32)],
                [xs_s, xq_s],
                [terms, d_hi, d_lo, neighbour, stiff, star, proj, lflux, own_lift, cluster],
            )
        elif odd_step:
            nsum, base = call(
                side,
                [nsum_s, base_s],
                [((3 * NBK, thin_columns), BF), ((192, thin_columns), BF)],
                [fresh, d_hi, d_lo, neighbour, stiff, thin_star, proj, thin_lflux, own_lift, cluster, nsum, base],
            )
        else:
            nsum, base = call(
                side,
                [nsum_s, base_s],
                [xs_s, xq_s],
                [terms, d_hi, d_lo, neighbour, stiff, star, proj, lflux, own_lift, cluster, nsum, base],
            )
        swapped = swapped.reshape(4, H, WIDE)
        swapped = jnp.where(holds_swapped, jnp.concatenate([swapped, swapped]), 0.0)
        p_rest = p_rest.reshape(8, 16, WIDE)
        block = jnp.concatenate([p_rest[:, 0:H], swapped], axis=1)
        block, nsum, base = lax.optimization_barrier((block, nsum, base))
        came = lax.cond(at_end, within_line, across_pair, block).reshape(128, WIDE)
    (out,) = call(
        functools.partial(critical, True, STEPS),
        [((NV, NB, E), F32)],
        [xg_s],
        [came, nsum, base, nflux, lift_a, lift_b, orient, far],
    )
    return jnp.transpose(out, (1, 0, 2))


def solution(mesh):
    placed = (
        P(None, None, ("dom", "sub")),
        P(),
        P(None, None, None, ("dom", "sub")),
        P(None, None, None, ("dom", "sub")),
        P(None, None, None, ("dom", "sub")),
        P(),
        P(),
        P(("dom", "sub")),
        P(None, ("dom", "sub")),
        P(None, ("dom", "sub")),
        P("dom", "sub", None),
    )
    return jax.shard_map(
        body, mesh=mesh, in_specs=placed, out_specs=P(None, None, ("dom", "sub")), check_vma=False
    )
```

```python
import functools

import jax
import jax.numpy as jnp
from jax import lax
from jax.experimental import pallas as pl
from jax.experimental.pallas import tpu as pltpu
from jax.sharding import PartitionSpec as P

ORDER = 5
STEPS = 8
NB = 35
NBP = 40
NBK = 48
NF = 15
NFP = 16
NV = 9
E = 128
H = 8
SLOTS = 96
FACES = 4 * E
WIDE = NV * NFP
COLS = NV * E
FACT = [1.0, 1.0, 2.0, 6.0, 24.0, 120.0, 720.0]
BF = jnp.bfloat16
F32 = jnp.float32


def halves(x):
    hi = x.astype(BF)
    lo = (x - hi.astype(F32)).astype(BF)
    return hi, lo


def dot(a, b):
    return jnp.dot(a, b, preferred_element_type=F32)


def fill_basis(xs_ref, values):
    pad = jnp.zeros((NBK - NBP, E), F32)
    for v in range(len(values)):
        hi, lo = halves(jnp.concatenate([values[v], pad], axis=0))
        cols = slice(v * E, (v + 1) * E)
        xs_ref[0:NBK, cols] = hi
        xs_ref[NBK : 2 * NBK, cols] = lo
        xs_ref[2 * NBK : 3 * NBK, cols] = hi


def derive(values, stiff_ref, star_ref, xs_ref):
    fill_basis(xs_ref, values)
    stiff = stiff_ref[...]
    chunks = [range(0, 4), range(4, 8), range(8, 9)]
    applied = [dot(stiff, xs_ref[:, c[0] * E : (c[-1] + 1) * E]) for c in chunks]
    acc = [None] * NV
    for chunk, piece in zip(chunks, applied):
        for d in range(3):
            for n, u in enumerate(chunk):
                part = piece[d * NBP : (d + 1) * NBP, n * E : (n + 1) * E]
                for v in range(NV):
                    term = part * star_ref[u, v, d : d + 1, :]
                    acc[v] = term if acc[v] is None else acc[v] + term
    return acc


def gather(got_ref, row_codes):
    got = jnp.concatenate(halves(got_ref[...]), axis=0)
    rows = lax.broadcasted_iota(jnp.int32, (128, E), 0)
    far = jnp.concatenate([(rows == row).astype(F32).astype(BF) for row in row_codes], axis=1)
    far = jnp.concatenate([far, far], axis=0)
    return lax.dot_general(got, far, (((0,), (0,)), ((), ())), preferred_element_type=F32)


def lane_group(shape):
    return lax.broadcasted_iota(jnp.int32, shape, len(shape) - 1) >> 5


def shifted(x, groups):
    return x if groups % 4 == 0 else pltpu.roll(x, groups % 4 * 32, x.ndim - 1)


def side_by_side(values):
    group = lane_group(values[0].shape)
    parts = []
    for j in range(3):
        part = jnp.zeros_like(values[0])
        for g in range(min(4, len(values) - 4 * j)):
            part = jnp.where(group == g, shifted(values[4 * j + g], g), part)
        parts.append(part)
    return parts


def apart(parts):
    return [shifted(parts[v // 4], -(v % 4)) for v in range(NV)]


def faces_side_by_side(rows):
    group = lane_group((1, E))
    joined = rows[0:1, :]
    for i in range(1, 4):
        joined = jnp.where(group == i, shifted(rows[i : i + 1, :], i), joined)
    return joined


def thin_matrices(full_ref, thin_ref):
    picks = []
    for to in range(2):
        for of in range(2):
            for r in range(4):
                picks.append([(4 * of + (g - r) % 4, 4 * to + g) for g in range(4)])
    picks += [[(8, g) for g in range(4)], [(8, 4 + g) for g in range(4)]]
    picks += [[(g, 8) for g in range(4)], [(4 + g, 8) for g in range(4)], [(8, 8)]]
    depth = full_ref.shape[2]
    group = lane_group((depth, E))
    for n, sources in enumerate(picks):
        row = jnp.zeros((depth, E), F32)
        for g, (u, v) in enumerate(sources):
            row = jnp.where(group == g, shifted(full_ref[u, v], g), row)
        thin_ref[n] = row


def mix(acc, parts, thin_ref, d):
    first, second, third = parts
    spread = third + shifted(third, 1)
    spread = spread + shifted(spread, 2)
    terms = [[], [], []]
    for r in range(4):
        one, two = shifted(first, r), shifted(second, r)
        for to in range(2):
            terms[to].append(one * thin_ref[8 * to + r, d : d + 1, :])
            terms[to].append(two * thin_ref[8 * to + 4 + r, d : d + 1, :])
    for to in range(2):
        terms[to].append(spread * thin_ref[16 + to, d : d + 1, :])
    terms[2] = [part * thin_ref[18 + n, d : d + 1, :] for n, part in enumerate(parts)]
    for to in range(3):
        for term in terms[to]:
            acc[to] = term if acc[to] is None else acc[to] + term


def mixed_parts(acc):
    last = acc[2] + shifted(acc[2], 2)
    last = last + shifted(last, 1)
    return [acc[0], acc[1], jnp.where(lane_group(last.shape) == 0, last, 0.0)]


def derive_thin(parts, stiff_ref, thin_ref, xt_ref):
    fill_basis(xt_ref, parts)
    applied = dot(stiff_ref[...], xt_ref[...])
    acc = [None] * 3
    for d in range(3):
        rows = applied[d * NBP : (d + 1) * NBP]
        mix(acc, [rows[:, j * E : (j + 1) * E] for j in range(3)], thin_ref, d)
    return mixed_parts(acc)


def weight_rows(cluster_ref, step):
    period = jnp.left_shift(jnp.int32(1), cluster_ref[...])
    offset = jnp.bitwise_and(jnp.int32(step), period - 1)
    a, inverse = offset.astype(F32), 1.0 / period.astype(F32)
    low, high, scale, rows = jnp.ones_like(a), jnp.ones_like(a), jnp.ones_like(a), []
    for k in range(ORDER):
        low, high = low * a, high * (a + 1.0)
        rows.append((high - low) * scale * (1.0 / FACT[k + 1]))
        scale = scale * inverse
    return rows, offset == 0


def expand_thin(step, current, cluster, stiff, thin, proj, pick, terms_in, terms, d_hi, d_lo, pay_swap, pay_rest, xs, xt):
    rows, start = weight_rows(cluster, step)
    fresh = [None] * 3
    for k in range(ORDER):
        if k > 0:
            current = derive_thin(current, stiff, thin, xt)
        for j in range(3):
            terms[k, j] = current[j]
            part = current[j] * (1.0 / FACT[k + 1])
            fresh[j] = part if k == 0 else fresh[j] + part
    fresh = apart(fresh)
    total = []
    for v in range(NV):
        kept = terms_in[0, v] * rows[0]
        for k in range(1, ORDER):
            kept = kept + terms_in[k, v] * rows[k]
        total.append(jnp.where(start, fresh[v], kept))
    send(total, proj, pick, d_hi, d_lo, pay_swap, pay_rest, xs)


def expand(step, first, upd, cluster, stiff, star, proj, pick, terms_in, terms, d_hi, d_lo, pay_swap, pay_rest, xs):
    rows, start = weight_rows(cluster, step)
    current = upd
    total = [None] * NV
    for k in range(ORDER):
        if k > 0:
            current = derive(current, stiff, star, xs)
        for v in range(NV):
            kept = current[v] if first else jnp.where(start, current[v], terms_in[k, v])
            terms[k, v] = kept
            part = kept * rows[k]
            total[v] = part if k == 0 else total[v] + part
    send(total, proj, pick, d_hi, d_lo, pay_swap, pay_rest, xs)


def send(total, proj, pick, d_hi, d_lo, pay_swap, pay_rest, xs):
    fill_basis(xs, total)
    faces = dot(proj[...], xs[...])
    for i in range(4):
        for v in range(NV):
            hi, lo = halves(faces[i * NFP : (i + 1) * NFP, v * E : (v + 1) * E])
            d_hi[v * NFP : (v + 1) * NFP, i * E : (i + 1) * E] = hi
            d_lo[v * NFP : (v + 1) * NFP, i * E : (i + 1) * E] = lo
    dims = (((1,), (1,)), ((), ()))
    pay = lax.dot_general(pick[...], d_hi[...], dims, preferred_element_type=F32)
    pay = pay + lax.dot_general(pick[...], d_lo[...], dims, preferred_element_type=F32)
    pay_swap[...] = pay[0:32]
    pay_rest[...] = pay[32:160]


def opening(*refs):
    raw, refs = refs[:11], list(refs[11:])
    take = lambda n: [refs.pop(0) for _ in range(n)]
    odd_ref = refs.pop(0)
    neighbour_ref, cluster, orient = take(3)
    stiff, proj, star, nflux, lflux, lift_a, lift_b, own_lift, pick, small = take(10)
    terms, d_hi, d_lo, pay_swap, pay_rest = take(5)
    dofs_s, stiff_s, proj_s, rot_s, send_ref, state, wide_s, tall_s, xs, sems = take(10)
    targets = [send_ref, neighbour_ref, stiff_s, proj_s, rot_s, cluster, dofs_s, star, nflux, lflux, orient]
    copies = [pltpu.make_async_copy(raw[n], targets[n], sems.at[n]) for n in range(11)]
    for copy in copies:
        copy.start()
    for copy in copies[:2]:
        copy.wait()

    high = lax.Precision.HIGHEST
    columns_first = (((0,), (0,)), ((), ()))

    def grid(shape):
        return lax.broadcasted_iota(jnp.int32, shape, 0), lax.broadcasted_iota(jnp.int32, shape, 1)

    odd = odd_ref[...]
    codes = neighbour_ref[...]
    slot = jnp.right_shift(codes - FACES, 2)
    block, source, place = slot >> 5, jnp.bitwise_and(slot >> 3, 3), jnp.bitwise_and(slot, 7)
    same, cross = 4 * (1 - odd), 4 * odd
    row = jnp.where(block == 2 * (1 - odd), (cross + source) * 16 + place, (same + source) * 16 + place)
    row = jnp.where(block == 2 * odd, row + H, row)
    row = jnp.where((codes >= FACES) & (codes < FACES + 4 * SLOTS), row, -1)
    small[8:12, :] = row
    small[0:1, :] = faces_side_by_side(codes)
    small[5:6, :] = faces_side_by_side(row)
    rows, columns = grid((160, SLOTS))
    flag = odd[:, 0:1]
    rest = rows - 32
    peer, place = rest >> 4, jnp.bitwise_and(rest, 15)
    inside = jnp.where((peer >> 2) == 1 - flag, 32, 64 * flag)
    wanted = inside + jnp.bitwise_and(peer, 3) * H + place
    wanted = jnp.where(rest < 0, 64 * (1 - flag) + rows, jnp.where(place < H, wanted, -1))
    chooser = (columns == wanted).astype(F32)
    listed = jnp.broadcast_to(send_ref[...].astype(F32), (8, SLOTS))
    listed = lax.dot_general(chooser, listed, (((1,), (1,)), ((), ())), precision=high, preferred_element_type=F32)
    listed = jnp.where(wanted[:, 0:1] < 0, float(FACES), listed[:, 0:1])
    _, columns = grid((160, FACES))
    pick[...] = (columns.astype(F32) == listed).astype(F32).astype(BF)

    for copy in copies[2:5]:
        copy.wait()
    wide_s[...] = jnp.zeros_like(wide_s)
    for d in range(3):
        wide_s[d * NBP : d * NBP + NB, 0:NB] = -stiff_s[d]
    rows, columns = grid((NBK, 3 * NBK))
    twice = ((columns == rows) | (columns == rows + NBK)).astype(F32).astype(BF)
    once = (columns == rows + 2 * NBK).astype(F32).astype(BF)
    hi, lo = halves(wide_s[...])
    stiff[...] = (dot(hi, twice) + dot(lo, once)).astype(BF)
    tall_s[...] = jnp.zeros_like(tall_s)
    for i in range(4):
        for f in range(NF):
            tall_s[i * NFP + f : i * NFP + f + 1, 0:NB] = proj_s[f, i : i + 1, :]
    hi, lo = halves(tall_s[...])
    proj[...] = (dot(hi, twice) + dot(lo, once)).astype(BF)
    rows, columns = grid((64, 192))
    twice = ((columns == rows) | (columns == rows + 64)).astype(F32).astype(BF)
    once = (columns == rows + 128).astype(F32).astype(BF)
    own = lax.dot_general(hi, twice, columns_first, preferred_element_type=F32)
    own = own + lax.dot_general(lo, once, columns_first, preferred_element_type=F32)
    own_lift[...] = own[0:NBP].astype(BF)
    mixed = jnp.zeros((64, 192), F32)
    to_rows, to_columns = grid((64, NF))
    from_rows, from_columns = grid((NF, 192))
    for o in range(3):
        spread = (jnp.bitwise_and(to_rows, 15) == to_columns).astype(F32)
        spread = jnp.dot(spread, rot_s[o], precision=high, preferred_element_type=F32)
        group = from_columns // 48
        placed = (from_columns - 48 * group == o * NFP + from_rows).astype(F32)
        mixed = mixed + jnp.dot(spread, placed, precision=high, preferred_element_type=F32)
    mixed = jnp.where((rows >> 4) == columns // 48, mixed, 0.0)
    lift = lax.dot_general(tall_s[...], mixed, columns_first, precision=high, preferred_element_type=F32)
    hi, lo = halves(lift[0:NBP])
    lift_a[0:NBP, :] = hi
    lift_a[NBP : 2 * NBP, :] = lo
    lift_b[...] = hi

    for copy in copies[5:]:
        copy.wait()
    for i in range(4):
        turns = jnp.where(lane_group((1, E)) == 0, orient[i : i + 1, :], 0)
        turns = turns + shifted(turns, 1)
        small[1 + i : 2 + i, :] = turns + shifted(turns, 2)
    state[...] = jnp.zeros_like(state)
    for v in range(NV):
        state[v, 0:NB, :] = dofs_s[v]
    upd = [state[v] for v in range(NV)]
    expand(0, True, upd, cluster, stiff, star, proj, pick, None, terms, d_hi, d_lo, pay_swap, pay_rest, xs)


def critical(last, step, *refs):
    refs = list(refs)
    take = lambda n: [refs.pop(0) for _ in range(n)]
    got_ref, nsum_ref, base_ref, nflux, lift_a, lift_b, orient, small = take(8)
    if last:
        out_ref, xg = take(2)
    else:
        stiff, star, proj, pick, cluster, terms_in = take(6)
        nsum_out, terms, d_hi, d_lo, pay_swap, pay_rest, xg, xs = take(8)

    total = nsum_ref[...] + gather(got_ref, [small[8 + i : 9 + i, :] for i in range(4)])
    if not last:
        nsum_out[...] = total
    for i in range(4):
        acc = [None] * NV
        for u in range(NV):
            part = total[u * NFP : (u + 1) * NFP, i * E : (i + 1) * E]
            for v in range(NV):
                term = part * nflux[u, v, i : i + 1, :]
                acc[v] = term if acc[v] is None else acc[v] + term
        chosen = []
        for o in range(3):
            mask = (orient[i : i + 1, :] == o).astype(F32)
            chosen.append(jnp.broadcast_to(mask, (NFP, E)).astype(BF))
        for v in range(NV):
            hi, lo = halves(acc[v])
            for o in range(3):
                row = (i * 3 + o) * NFP
                cols = slice(v * E, (v + 1) * E)
                xg[row : row + NFP, cols] = hi * chosen[o]
                xg[192 + row : 192 + row + NFP, cols] = lo * chosen[o]
    two = dot(lift_a[...], xg[0:192, :])
    lifted = two[0:NBP] + two[NBP : 2 * NBP] + dot(lift_b[...], xg[192:384, :])
    upd = [base_ref[v] + lifted[:, v * E : (v + 1) * E] for v in range(NV)]
    if last:
        for v in range(NV):
            out_ref[v] = upd[v][0:NB]
    else:
        expand(step, False, upd, cluster, stiff, star, proj, pick, terms_in, terms, d_hi, d_lo, pay_swap, pay_rest, xs)


def critical_thin(step, *refs):
    got_ref, nsum_ref, base_ref, nflux, lift_a, lift_b, small, stiff, star, proj, pick, cluster, terms_in = refs[:13]
    terms, d_hi, d_lo, pay_swap, pay_rest, xg, xs, xt = refs[13:]
    total = nsum_ref[...] + gather(got_ref, [small[5:6, :]])
    acc = [None] * NV
    for u in range(NV):
        part = total[u * NFP : (u + 1) * NFP, :]
        for v in range(NV):
            term = part * nflux[u * NV + v : u * NV + v + 1, :]
            acc[v] = term if acc[v] is None else acc[v] + term
    group = lane_group((NFP, E))
    for i in range(4):
        chosen = []
        for o in range(3):
            mask = (small[1 + i : 2 + i, :] == o).astype(F32)
            chosen.append(jnp.broadcast_to(mask, (NFP, E)).astype(BF))
        for j in range(3):
            part = jnp.zeros((NFP, E), F32)
            for g in range(min(4, NV - 4 * j)):
                part = jnp.where(group == g, shifted(acc[4 * j + g], g - i), part)
            hi, lo = halves(part)
            cols = slice(j * E, (j + 1) * E)
            for o in range(3):
                row = (i * 3 + o) * NFP
                xg[row : row + NFP, cols] = hi * chosen[o]
                xg[192 + row : 192 + row + NFP, cols] = lo * chosen[o]
    two = dot(lift_a[...], xg[0:192, :])
    lifted = two[0:NBP] + two[NBP : 2 * NBP] + dot(lift_b[...], xg[192:384, :])
    base = side_by_side([base_ref[v] for v in range(NV)])
    upd = [base[j] + lifted[:, j * E : (j + 1) * E] for j in range(3)]
    expand_thin(step, upd, cluster, stiff, star, proj, pick, terms_in, terms, d_hi, d_lo, pay_swap, pay_rest, xs, xt)


def beside(step, *refs):
    refs = list(refs)
    take = lambda n: [refs.pop(0) for _ in range(n)]
    first, thin = step == 0, step % 2 == 1
    terms, d_hi, d_lo, neighbour, stiff, star, proj, lflux, own_lift, cluster = take(10)
    small = refs.pop(0)
    if thin:
        got_ref = refs.pop(0)
    if first:
        nflux = refs.pop(0)
    else:
        nsum_ref, base_ref = take(2)
    nsum_out, base_out = take(2)
    if not thin:
        nsum_thin = refs.pop(0)
    if first:
        thin_star, thin_lflux, thin_nflux = take(3)
    xs, xq = take(2)
    _, start = weight_rows(cluster, step)
    period = jnp.left_shift(jnp.int32(1), cluster[...]).astype(F32)
    face_rows = lax.broadcasted_iota(jnp.int32, (FACES, E), 0)
    if thin:
        arrived = gather(got_ref, [small[8 + i : 9 + i, :] for i in range(4)])
    for i in range(4):
        cols = slice(i * E, (i + 1) * E)
        near = (face_rows == neighbour[i : i + 1, :]).astype(F32).astype(BF)
        gathered = dot(d_hi[...], near) + dot(d_lo[...], near)
        if not first:
            kept = nsum_ref[:, cols]
            if thin:
                kept = kept + arrived[:, cols]
            gathered = gathered + jnp.where(start, 0.0, kept)
        nsum_out[:, cols] = gathered
    if not thin:
        near = (face_rows == small[0:1, :]).astype(F32).astype(BF)
        nsum_thin[...] = dot(d_hi[...], near) + dot(d_lo[...], near)
    wide = 3 if thin else NV
    held = [[terms[k, v] for v in range(wide)] for k in range(ORDER)]
    if thin:
        final = derive_thin(held[ORDER - 1], stiff, star, xs)
    else:
        final = derive(held[ORDER - 1], stiff, star, xs)
    state = []
    whole = []
    for v in range(wide):
        volume = final[v] * (1.0 / FACT[ORDER])
        own = held[0][v]
        for k in range(1, ORDER):
            volume = volume + held[k][v] * (1.0 / FACT[k])
            own = own + held[k][v] * (1.0 / FACT[k + 1])
        state.append(held[0][v] + volume)
        whole.append(own if thin else own * period)
    fill_basis(xs, whole)
    faces = dot(proj[...], xs[...])
    for i in range(4):
        rows = faces[i * NFP : (i + 1) * NFP]
        acc = [None] * wide
        if thin:
            mix(acc, [rows[:, j * E : (j + 1) * E] for j in range(3)], lflux, i)
            acc = mixed_parts(acc)
        else:
            for u in range(NV):
                part = rows[:, u * E : (u + 1) * E]
                for v in range(NV):
                    term = part * lflux[u, v, i : i + 1, :]
                    acc[v] = term if acc[v] is None else acc[v] + term
        for v in range(wide):
            hi, lo = halves(acc[v])
            cols = slice(v * E, (v + 1) * E)
            xq[i * NFP : (i + 1) * NFP, cols] = hi
            xq[64 + i * NFP : 64 + (i + 1) * NFP, cols] = lo
            xq[128 + i * NFP : 128 + (i + 1) * NFP, cols] = hi
    lifted = dot(own_lift[...], xq[...])
    fresh = [state[v] - lifted[:, v * E : (v + 1) * E] for v in range(wide)]
    if thin:
        fresh = apart(fresh)
    for v in range(NV):
        base_out[v] = fresh[v] if first else jnp.where(start, fresh[v], base_ref[v])
    if first:
        thin_matrices(star, thin_star)
        thin_matrices(lflux, thin_lflux)
        for u in range(NV):
            for v in range(NV):
                thin_nflux[u * NV + v : u * NV + v + 1, :] = faces_side_by_side(nflux[u, v])


def call(kernel, outs, scratch, args, raw=0):
    def memory(s):
        return pltpu.VMEM(*s) if isinstance(s, tuple) else s

    return pl.pallas_call(
        kernel,
        out_shape=[jax.ShapeDtypeStruct(s, t) for s, t in outs],
        in_specs=[pl.BlockSpec(memory_space=pltpu.HBM if n < raw else pltpu.VMEM) for n in range(len(args))],
        out_specs=[pl.BlockSpec(memory_space=pltpu.VMEM)] * len(outs),
        scratch_shapes=[memory(s) for s in scratch],
        compiler_params=pltpu.CompilerParams(vmem_limit_bytes=40 * 1024 * 1024),
    )(*args)


def body(dofs, stiffness, star, local_flux, neighbour_flux, face_proj, face_rot, cluster, neighbour, orient, send_list):
    n_dom, n_sub = lax.axis_size("dom"), lax.axis_size("sub")
    odd = lax.axis_index("dom") % 2
    chip = [(i, i ^ 1) for i in range(n_dom)]
    groups = [
        [(i + h) % n_dom * n_sub + t for h in range(2) for t in range(n_sub)] for i in range(1, n_dom, 2)
    ]
    lines = [[i * n_sub + t for t in range(n_sub)] for i in range(n_dom)]
    dom = lax.axis_index("dom")
    at_end = (dom == 0) | (dom == n_dom - 1)

    def exchange(block, among):
        return lax.all_to_all(
            block, ("dom", "sub"), split_axis=0, concat_axis=0, tiled=True, axis_index_groups=among
        )

    def across_pair(block):
        return exchange(block, groups)

    def within_line(block):
        own = exchange(jnp.where(odd == 1, block[0:4], block[4:8]), lines)
        return jnp.concatenate([own, own])

    holds_swapped = (jnp.arange(8, dtype=jnp.int32) // 4 == 1 - odd)[:, None, None]
    raw = [
        send_list.reshape(1, SLOTS),
        neighbour,
        stiffness,
        jnp.transpose(face_proj, (1, 0, 2)),
        face_rot,
        cluster.reshape(1, E),
        jnp.transpose(dofs, (1, 0, 2)),
        jnp.transpose(star, (1, 2, 0, 3)),
        jnp.transpose(neighbour_flux, (1, 2, 0, 3)),
        jnp.transpose(local_flux, (1, 2, 0, 3)),
        orient,
    ]
    raw = [pltpu.with_memory_space_constraint(x, pltpu.HBM) for x in raw]
    flux_s = ((NV, NV, 4, E), F32)
    constants = [
        ((4, E), jnp.int32),
        ((1, E), jnp.int32),
        ((4, E), jnp.int32),
        ((3 * NBP, 3 * NBK), BF),
        ((4 * NFP, 3 * NBK), BF),
        ((NV, NV, 3, E), F32),
        flux_s,
        flux_s,
        ((2 * NBP, 192), BF),
        ((NBP, 192), BF),
        ((NBP, 192), BF),
        ((160, FACES), BF),
        ((16, E), jnp.int32),
    ]
    terms_s = ((ORDER, NV, NBP, E), F32)
    face_s = ((WIDE, FACES), BF)
    nsum_s = ((WIDE, FACES), F32)
    base_s = ((NV, NBP, E), F32)
    xs_s = ((3 * NBK, COLS), BF)
    xg_s = ((384, COLS), BF)
    xq_s = ((192, COLS), BF)
    sends = [terms_s, face_s, face_s, ((32, WIDE), F32), ((128, WIDE), F32)]
    fetched = [
        ((NV, NB, E), F32),
        ((3, NB, NB), F32),
        ((NF, 4, NB), F32),
        ((3, NF, NF), F32),
        ((1, SLOTS), jnp.int32),
        base_s,
        ((3 * NBP, NBK), F32),
        ((4 * NFP, NBK), F32),
        xs_s,
        pltpu.SemaphoreType.DMA((11,)),
    ]
    begun = call(
        opening,
        constants + sends,
        fetched,
        raw + [jnp.full((1, E), odd, jnp.int32)],
        raw=11,
    )
    neighbour, cluster, orient = begun[:3]
    stiff, proj, star, nflux, lflux, lift_a, lift_b, own_lift, pick, small = begun[3:13]
    terms, d_hi, d_lo, p_swap, p_rest = begun[13:]
    thin_s = ((ORDER, 3, NBP, E), F32)
    thin_columns = 3 * E
    for step in range(STEPS):
        odd_step = step % 2 == 1
        if odd_step:
            fresh, d_hi, d_lo, p_swap, p_rest = call(
                functools.partial(critical_thin, step),
                [thin_s] + sends[1:],
                [((384, thin_columns), BF), xs_s, ((3 * NBK, thin_columns), BF)],
                [came, nsum_thin, base, thin_nflux, lift_a, lift_b, small]
                + [stiff, thin_star, proj, pick, cluster, terms],
            )
        elif step > 0:
            nsum, terms, d_hi, d_lo, p_swap, p_rest = call(
                functools.partial(critical, False, step),
                [nsum_s] + sends,
                [xg_s, xs_s],
                [came, nsum, base, nflux, lift_a, lift_b, orient, small, stiff, star, proj, pick, cluster, terms],
            )
        swapped = lax.ppermute(p_swap, "dom", chip)
        side = functools.partial(beside, step)
        thin_nsum_s = ((WIDE, E), F32)
        if step == 0:
            nsum, base, nsum_thin, thin_star, thin_lflux, thin_nflux = call(
                side,
                [nsum_s, base_s, thin_nsum_s, ((21, 3, E), F32), ((21, 4, E), F32), ((NV * NV, E), F32)],
                [xs_s, xq_s],
                [terms, d_hi, d_lo, neighbour, stiff, star, proj, lflux, own_lift, cluster, small, nflux],
            )
        elif odd_step:
            nsum, base = call(
                side,
                [nsum_s, base_s],
                [((3 * NBK, thin_columns), BF), ((192, thin_columns), BF)],
                [fresh, d_hi, d_lo, neighbour, stiff, thin_star, proj, thin_lflux, own_lift, cluster]
                + [small, came, nsum, base],
            )
        else:
            nsum, base, nsum_thin = call(
                side,
                [nsum_s, base_s, thin_nsum_s],
                [xs_s, xq_s],
                [terms, d_hi, d_lo, neighbour, stiff, star, proj, lflux, own_lift, cluster, small, nsum, base],
            )
        swapped = swapped.reshape(4, H, WIDE)
        swapped = jnp.where(holds_swapped, jnp.concatenate([swapped, swapped]), 0.0)
        p_rest = p_rest.reshape(8, 16, WIDE)
        block = jnp.concatenate([p_rest[:, 0:H], swapped], axis=1)
        if odd_step:
            block, nsum, base = lax.optimization_barrier((block, nsum, base))
        else:
            block, nsum, base, nsum_thin = lax.optimization_barrier((block, nsum, base, nsum_thin))
        came = lax.cond(at_end, within_line, across_pair, block).reshape(128, WIDE)
    (out,) = call(
        functools.partial(critical, True, STEPS),
        [((NV, NB, E), F32)],
        [xg_s],
        [came, nsum, base, nflux, lift_a, lift_b, orient, small],
    )
    return jnp.transpose(out, (1, 0, 2))


def solution(mesh):
    placed = (
        P(None, None, ("dom", "sub")),
        P(),
        P(None, None, None, ("dom", "sub")),
        P(None, None, None, ("dom", "sub")),
        P(None, None, None, ("dom", "sub")),
        P(),
        P(),
        P(("dom", "sub")),
        P(None, ("dom", "sub")),
        P(None, ("dom", "sub")),
        P("dom", "sub", None),
    )
    return jax.shard_map(
        body, mesh=mesh, in_specs=placed, out_specs=P(None, None, ("dom", "sub")), check_vma=False
    )
```

```python
import functools

import jax
import jax.numpy as jnp
from jax import lax
from jax.experimental import pallas as pl
from jax.experimental.pallas import tpu as pltpu
from jax.sharding import PartitionSpec as P

ORDER = 5
STEPS = 8
NB = 35
NBP = 40
NBK = 48
NF = 15
NFP = 16
NV = 9
E = 128
H = 8
SLOTS = 96
FACES = 4 * E
WIDE = NV * NFP
COLS = NV * E
FACT = [1.0, 1.0, 2.0, 6.0, 24.0, 120.0, 720.0]
BF = jnp.bfloat16
F32 = jnp.float32


def halves(x):
    hi = x.astype(BF)
    lo = (x - hi.astype(F32)).astype(BF)
    return hi, lo


def dot(a, b):
    return jnp.dot(a, b, preferred_element_type=F32)


def fill_basis(xs_ref, values):
    pad = jnp.zeros((NBK - NBP, E), F32)
    for v in range(len(values)):
        hi, lo = halves(jnp.concatenate([values[v], pad], axis=0))
        cols = slice(v * E, (v + 1) * E)
        xs_ref[0:NBK, cols] = hi
        xs_ref[NBK : 2 * NBK, cols] = lo
        xs_ref[2 * NBK : 3 * NBK, cols] = hi


def derive(values, stiff_ref, star_ref, xs_ref):
    fill_basis(xs_ref, values)
    stiff = stiff_ref[...]
    chunks = [range(0, 4), range(4, 8), range(8, 9)]
    applied = [dot(stiff, xs_ref[:, c[0] * E : (c[-1] + 1) * E]) for c in chunks]
    acc = [None] * NV
    for chunk, piece in zip(chunks, applied):
        for d in range(3):
            for n, u in enumerate(chunk):
                part = piece[d * NBP : (d + 1) * NBP, n * E : (n + 1) * E]
                for v in range(NV):
                    term = part * star_ref[u, v, d : d + 1, :]
                    acc[v] = term if acc[v] is None else acc[v] + term
    return acc


def gather(got_ref, row_codes):
    got = jnp.concatenate(halves(got_ref[...]), axis=0)
    rows = lax.broadcasted_iota(jnp.int32, (128, E), 0)
    far = jnp.concatenate([(rows == row).astype(F32).astype(BF) for row in row_codes], axis=1)
    far = jnp.concatenate([far, far], axis=0)
    return lax.dot_general(got, far, (((0,), (0,)), ((), ())), preferred_element_type=F32)


def lane_group(shape, g=4):
    return lax.broadcasted_iota(jnp.int32, shape, len(shape) - 1) // (E // g)


def shifted(x, groups, g=4):
    return x if groups % g == 0 else pltpu.roll(x, groups % g * (E // g), x.ndim - 1)


def side_by_side(values, g=4):
    group = lane_group(values[0].shape, g)
    parts = []
    for j in range(-(-NV // g)):
        part = jnp.zeros_like(values[0])
        for n in range(min(g, NV - g * j)):
            part = jnp.where(group == n, shifted(values[g * j + n], n, g), part)
        parts.append(part)
    return parts


def apart(parts, g=4):
    return [shifted(parts[v // g], -(v % g), g) for v in range(NV)]


def over_groups(x, g):
    for distance in (1, 2)[: g // 2]:
        x = x + shifted(x, distance, g)
    return x


def faces_side_by_side(rows):
    group = lane_group((1, E))
    joined = rows[0:1, :]
    for i in range(1, 4):
        joined = jnp.where(group == i, shifted(rows[i : i + 1, :], i), joined)
    return joined


def thin_matrices(full_ref, thin_ref, g=4):
    whole = NV // g
    picks = []
    for to in range(whole):
        for of in range(whole):
            for r in range(g):
                picks.append([(g * of + (n - r) % g, g * to + n) for n in range(g)])
    picks += [[(NV - 1, g * to + n) for n in range(g)] for to in range(whole)]
    picks += [[(g * of + n, NV - 1) for n in range(g)] for of in range(whole)]
    picks.append([(NV - 1, NV - 1)])
    depth = full_ref.shape[2]
    group = lane_group((depth, E), g)
    for k, sources in enumerate(picks):
        row = jnp.zeros((depth, E), F32)
        for n, (u, v) in enumerate(sources):
            row = jnp.where(group == n, shifted(full_ref[u, v], n, g), row)
        thin_ref[k] = row


def mix(acc, parts, thin_ref, d, g=4):
    whole = NV // g
    spread = over_groups(parts[whole], g)
    terms = [[] for _ in range(whole)]
    for of in range(whole):
        for r in range(g):
            part = shifted(parts[of], r, g)
            for to in range(whole):
                terms[to].append(part * thin_ref[(to * whole + of) * g + r, d : d + 1, :])
    base = whole * whole * g
    for to in range(whole):
        terms[to].append(spread * thin_ref[base + to, d : d + 1, :])
    base = base + whole
    terms.append([part * thin_ref[base + n, d : d + 1, :] for n, part in enumerate(parts)])
    for to in range(whole + 1):
        for term in terms[to]:
            acc[to] = term if acc[to] is None else acc[to] + term


def mixed_parts(acc, g=4):
    last = over_groups(acc[-1], g)
    return acc[:-1] + [jnp.where(lane_group(last.shape, g) == 0, last, 0.0)]


def derive_thin(parts, stiff_ref, thin_ref, xt_ref, g=4):
    fill_basis(xt_ref, parts)
    applied = dot(stiff_ref[...], xt_ref[:, 0 : len(parts) * E])
    acc = [None] * len(parts)
    for d in range(3):
        rows = applied[d * NBP : (d + 1) * NBP]
        mix(acc, [rows[:, j * E : (j + 1) * E] for j in range(len(parts))], thin_ref, d, g)
    return mixed_parts(acc, g)


def weight_rows(cluster_ref, step):
    period = jnp.left_shift(jnp.int32(1), cluster_ref[...])
    offset = jnp.bitwise_and(jnp.int32(step), period - 1)
    a, inverse = offset.astype(F32), 1.0 / period.astype(F32)
    low, high, scale, rows = jnp.ones_like(a), jnp.ones_like(a), jnp.ones_like(a), []
    for k in range(ORDER):
        low, high = low * a, high * (a + 1.0)
        rows.append((high - low) * scale * (1.0 / FACT[k + 1]))
        scale = scale * inverse
    return rows, offset == 0


def expand_thin(step, current, cluster, stiff, thin, proj, pick, terms_in, terms, d_hi, d_lo, pay_swap, pay_rest, xs, xt):
    rows, start = weight_rows(cluster, step)
    fresh = [None] * 3
    for k in range(ORDER):
        if k > 0:
            current = derive_thin(current, stiff, thin, xt)
        for j in range(3):
            terms[k, j] = current[j]
            part = current[j] * (1.0 / FACT[k + 1])
            fresh[j] = part if k == 0 else fresh[j] + part
    fresh = apart(fresh)
    total = []
    for v in range(NV):
        kept = terms_in[0, v] * rows[0]
        for k in range(1, ORDER):
            kept = kept + terms_in[k, v] * rows[k]
        total.append(jnp.where(start, fresh[v], kept))
    send(total, proj, pick, d_hi, d_lo, pay_swap, pay_rest, xs)


def expand(step, first, upd, cluster, stiff, star, proj, pick, terms_in, terms, d_hi, d_lo, pay_swap, pay_rest, xs):
    rows, start = weight_rows(cluster, step)
    paired = step % 4 == 2
    current = upd
    total = [None] * NV
    for k in range(ORDER):
        if paired:
            parts = side_by_side(upd, 2) if k == 0 else derive_thin(parts, stiff, star, xs, 2)
            current = upd if k == 0 else apart(parts, 2)
        elif k > 0:
            current = derive(current, stiff, star, xs)
        for v in range(NV):
            kept = current[v] if first else jnp.where(start, current[v], terms_in[k, v])
            terms[k, v] = kept
            part = kept * rows[k]
            total[v] = part if k == 0 else total[v] + part
    send(total, proj, pick, d_hi, d_lo, pay_swap, pay_rest, xs)


def send(total, proj, pick, d_hi, d_lo, pay_swap, pay_rest, xs):
    fill_basis(xs, total)
    faces = dot(proj[...], xs[...])
    for i in range(4):
        for v in range(NV):
            hi, lo = halves(faces[i * NFP : (i + 1) * NFP, v * E : (v + 1) * E])
            d_hi[v * NFP : (v + 1) * NFP, i * E : (i + 1) * E] = hi
            d_lo[v * NFP : (v + 1) * NFP, i * E : (i + 1) * E] = lo
    dims = (((1,), (1,)), ((), ()))
    pay = lax.dot_general(pick[...], d_hi[...], dims, preferred_element_type=F32)
    pay = pay + lax.dot_general(pick[...], d_lo[...], dims, preferred_element_type=F32)
    pay_swap[...] = pay[0:32]
    pay_rest[...] = pay[32:96]


def opening(*refs):
    raw, refs = refs[:11], list(refs[11:])
    take = lambda n: [refs.pop(0) for _ in range(n)]
    odd_ref = refs.pop(0)
    neighbour_ref, cluster, orient = take(3)
    stiff, proj, star, nflux, lflux, lift_a, lift_b, own_lift, pick, small = take(10)
    terms, d_hi, d_lo, pay_swap, pay_rest = take(5)
    dofs_s, stiff_s, proj_s, rot_s, send_ref, state, wide_s, tall_s, xs, sems = take(10)
    targets = [send_ref, neighbour_ref, stiff_s, proj_s, rot_s, cluster, dofs_s, star, nflux, lflux, orient]
    copies = [pltpu.make_async_copy(raw[n], targets[n], sems.at[n]) for n in range(11)]
    for copy in copies:
        copy.start()
    for copy in copies[:2]:
        copy.wait()

    high = lax.Precision.HIGHEST
    columns_first = (((0,), (0,)), ((), ()))

    def grid(shape):
        return lax.broadcasted_iota(jnp.int32, shape, 0), lax.broadcasted_iota(jnp.int32, shape, 1)

    odd = odd_ref[...]
    codes = neighbour_ref[...]
    slot = jnp.right_shift(codes - FACES, 2)
    block, source, place = slot >> 5, jnp.bitwise_and(slot >> 3, 3), jnp.bitwise_and(slot, 7)
    same, cross = 4 * (1 - odd), 4 * odd
    row = jnp.where(block == 2 * (1 - odd), (cross + source) * 16 + place, (same + source) * 16 + place)
    row = jnp.where(block == 2 * odd, row + H, row)
    row = jnp.where((codes >= FACES) & (codes < FACES + 4 * SLOTS), row, -1)
    small[8:12, :] = row
    small[0:1, :] = faces_side_by_side(codes)
    small[5:6, :] = faces_side_by_side(row)
    rows, columns = grid((96, SLOTS))
    flag = odd[:, 0:1]
    rest = rows - 32
    peer, place = rest >> 3, jnp.bitwise_and(rest, 7)
    inside = jnp.where((peer >> 2) == 1 - flag, 32, 64 * flag)
    wanted = inside + jnp.bitwise_and(peer, 3) * H + place
    wanted = jnp.where(rest < 0, 64 * (1 - flag) + rows, wanted)
    chooser = (columns == wanted).astype(F32)
    listed = jnp.broadcast_to(send_ref[...].astype(F32), (8, SLOTS))
    listed = lax.dot_general(chooser, listed, (((1,), (1,)), ((), ())), precision=high, preferred_element_type=F32)
    _, columns = grid((96, FACES))
    pick[...] = (columns.astype(F32) == listed[:, 0:1]).astype(F32).astype(BF)

    for copy in copies[2:5]:
        copy.wait()
    wide_s[...] = jnp.zeros_like(wide_s)
    for d in range(3):
        wide_s[d * NBP : d * NBP + NB, 0:NB] = -stiff_s[d]
    rows, columns = grid((NBK, 3 * NBK))
    twice = ((columns == rows) | (columns == rows + NBK)).astype(F32).astype(BF)
    once = (columns == rows + 2 * NBK).astype(F32).astype(BF)
    hi, lo = halves(wide_s[...])
    stiff[...] = (dot(hi, twice) + dot(lo, once)).astype(BF)
    tall_s[...] = jnp.zeros_like(tall_s)
    for i in range(4):
        for f in range(NF):
            tall_s[i * NFP + f : i * NFP + f + 1, 0:NB] = proj_s[f, i : i + 1, :]
    hi, lo = halves(tall_s[...])
    proj[...] = (dot(hi, twice) + dot(lo, once)).astype(BF)
    for copy in copies[5:8]:
        copy.wait()
    state[...] = jnp.zeros_like(state)
    for v in range(NV):
        state[v, 0:NB, :] = dofs_s[v]
    upd = [state[v] for v in range(NV)]
    expand(0, True, upd, cluster, stiff, star, proj, pick, None, terms, d_hi, d_lo, pay_swap, pay_rest, xs)

    rows, columns = grid((64, 192))
    twice = ((columns == rows) | (columns == rows + 64)).astype(F32).astype(BF)
    once = (columns == rows + 128).astype(F32).astype(BF)
    own = lax.dot_general(hi, twice, columns_first, preferred_element_type=F32)
    own = own + lax.dot_general(lo, once, columns_first, preferred_element_type=F32)
    own_lift[...] = own[0:NBP].astype(BF)
    mixed = jnp.zeros((64, 192), F32)
    to_rows, to_columns = grid((64, NF))
    from_rows, from_columns = grid((NF, 192))
    for o in range(3):
        spread = (jnp.bitwise_and(to_rows, 15) == to_columns).astype(F32)
        spread = jnp.dot(spread, rot_s[o], precision=high, preferred_element_type=F32)
        group = from_columns // 48
        placed = (from_columns - 48 * group == o * NFP + from_rows).astype(F32)
        mixed = mixed + jnp.dot(spread, placed, precision=high, preferred_element_type=F32)
    mixed = jnp.where((rows >> 4) == columns // 48, mixed, 0.0)
    lift = lax.dot_general(tall_s[...], mixed, columns_first, precision=high, preferred_element_type=F32)
    hi, lo = halves(lift[0:NBP])
    lift_a[0:NBP, :] = hi
    lift_a[NBP : 2 * NBP, :] = lo
    lift_b[...] = hi
    for copy in copies[8:]:
        copy.wait()
    for i in range(4):
        turns = jnp.where(lane_group((1, E)) == 0, orient[i : i + 1, :], 0)
        turns = turns + shifted(turns, 1)
        small[1 + i : 2 + i, :] = turns + shifted(turns, 2)


def critical(last, step, *refs):
    refs = list(refs)
    take = lambda n: [refs.pop(0) for _ in range(n)]
    got_ref, nsum_ref, base_ref, nflux, lift_a, lift_b, orient, small = take(8)
    if last:
        out_ref, xg = take(2)
    else:
        stiff, star, proj, pick, cluster, terms_in = take(6)
        nsum_out, terms, d_hi, d_lo, pay_swap, pay_rest, xg, xs = take(8)

    total = nsum_ref[...] + gather(got_ref, [small[8 + i : 9 + i, :] for i in range(4)])
    if not last:
        nsum_out[...] = total
    for i in range(4):
        acc = [None] * NV
        for u in range(NV):
            part = total[u * NFP : (u + 1) * NFP, i * E : (i + 1) * E]
            for v in range(NV):
                term = part * nflux[u, v, i : i + 1, :]
                acc[v] = term if acc[v] is None else acc[v] + term
        chosen = []
        for o in range(3):
            mask = (orient[i : i + 1, :] == o).astype(F32)
            chosen.append(jnp.broadcast_to(mask, (NFP, E)).astype(BF))
        for v in range(NV):
            hi, lo = halves(acc[v])
            for o in range(3):
                row = (i * 3 + o) * NFP
                cols = slice(v * E, (v + 1) * E)
                xg[row : row + NFP, cols] = hi * chosen[o]
                xg[192 + row : 192 + row + NFP, cols] = lo * chosen[o]
    two = dot(lift_a[...], xg[0:192, :])
    lifted = two[0:NBP] + two[NBP : 2 * NBP] + dot(lift_b[...], xg[192:384, :])
    upd = [base_ref[v] + lifted[:, v * E : (v + 1) * E] for v in range(NV)]
    if last:
        for v in range(NV):
            out_ref[v] = upd[v][0:NB]
    else:
        expand(step, False, upd, cluster, stiff, star, proj, pick, terms_in, terms, d_hi, d_lo, pay_swap, pay_rest, xs)


def critical_thin(step, *refs):
    got_ref, nsum_ref, base_ref, nflux, lift_a, lift_b, small, stiff, star, proj, pick, cluster, terms_in = refs[:13]
    terms, d_hi, d_lo, pay_swap, pay_rest, xg, xs, xt = refs[13:]
    total = nsum_ref[...] + gather(got_ref, [small[5:6, :]])
    acc = [None] * NV
    for u in range(NV):
        part = total[u * NFP : (u + 1) * NFP, :]
        for v in range(NV):
            term = part * nflux[u * NV + v : u * NV + v + 1, :]
            acc[v] = term if acc[v] is None else acc[v] + term
    group = lane_group((NFP, E))
    for i in range(4):
        chosen = []
        for o in range(3):
            mask = (small[1 + i : 2 + i, :] == o).astype(F32)
            chosen.append(jnp.broadcast_to(mask, (NFP, E)).astype(BF))
        for j in range(3):
            part = jnp.zeros((NFP, E), F32)
            for g in range(min(4, NV - 4 * j)):
                part = jnp.where(group == g, shifted(acc[4 * j + g], g - i), part)
            hi, lo = halves(part)
            cols = slice(j * E, (j + 1) * E)
            for o in range(3):
                row = (i * 3 + o) * NFP
                xg[row : row + NFP, cols] = hi * chosen[o]
                xg[192 + row : 192 + row + NFP, cols] = lo * chosen[o]
    two = dot(lift_a[...], xg[0:192, :])
    lifted = two[0:NBP] + two[NBP : 2 * NBP] + dot(lift_b[...], xg[192:384, :])
    base = side_by_side([base_ref[v] for v in range(NV)])
    upd = [base[j] + lifted[:, j * E : (j + 1) * E] for j in range(3)]
    expand_thin(step, upd, cluster, stiff, star, proj, pick, terms_in, terms, d_hi, d_lo, pay_swap, pay_rest, xs, xt)


def beside(step, *refs):
    refs = list(refs)
    take = lambda n: [refs.pop(0) for _ in range(n)]
    first, thin = step == 0, step % 2 == 1
    terms, d_hi, d_lo, neighbour, stiff, star, proj, lflux, own_lift, cluster = take(10)
    small = refs.pop(0)
    if thin:
        got_ref = refs.pop(0)
    if first:
        nflux = refs.pop(0)
    else:
        nsum_ref, base_ref = take(2)
    nsum_out, base_out = take(2)
    if not thin:
        nsum_thin = refs.pop(0)
    if first:
        thin_star, thin_lflux, thin_nflux, pair_star = take(4)
    xs, xq = take(2)
    _, start = weight_rows(cluster, step)
    period = jnp.left_shift(jnp.int32(1), cluster[...]).astype(F32)
    face_rows = lax.broadcasted_iota(jnp.int32, (FACES, E), 0)
    if thin:
        arrived = gather(got_ref, [small[8 + i : 9 + i, :] for i in range(4)])
    for i in range(4):
        cols = slice(i * E, (i + 1) * E)
        near = (face_rows == neighbour[i : i + 1, :]).astype(F32).astype(BF)
        gathered = dot(d_hi[...], near) + dot(d_lo[...], near)
        if not first:
            kept = nsum_ref[:, cols]
            if thin:
                kept = kept + arrived[:, cols]
            gathered = gathered + jnp.where(start, 0.0, kept)
        nsum_out[:, cols] = gathered
    if not thin:
        near = (face_rows == small[0:1, :]).astype(F32).astype(BF)
        nsum_thin[...] = dot(d_hi[...], near) + dot(d_lo[...], near)
    wide = 3 if thin else NV
    held = [[terms[k, v] for v in range(wide)] for k in range(ORDER)]
    if thin:
        final = derive_thin(held[ORDER - 1], stiff, star, xs)
    else:
        final = derive(held[ORDER - 1], stiff, star, xs)
    state = []
    whole = []
    for v in range(wide):
        volume = final[v] * (1.0 / FACT[ORDER])
        own = held[0][v]
        for k in range(1, ORDER):
            volume = volume + held[k][v] * (1.0 / FACT[k])
            own = own + held[k][v] * (1.0 / FACT[k + 1])
        state.append(held[0][v] + volume)
        whole.append(own if thin else own * period)
    fill_basis(xs, whole)
    faces = dot(proj[...], xs[...])
    for i in range(4):
        rows = faces[i * NFP : (i + 1) * NFP]
        acc = [None] * wide
        if thin:
            mix(acc, [rows[:, j * E : (j + 1) * E] for j in range(3)], lflux, i)
            acc = mixed_parts(acc)
        else:
            for u in range(NV):
                part = rows[:, u * E : (u + 1) * E]
                for v in range(NV):
                    term = part * lflux[u, v, i : i + 1, :]
                    acc[v] = term if acc[v] is None else acc[v] + term
        for v in range(wide):
            hi, lo = halves(acc[v])
            cols = slice(v * E, (v + 1) * E)
            xq[i * NFP : (i + 1) * NFP, cols] = hi
            xq[64 + i * NFP : 64 + (i + 1) * NFP, cols] = lo
            xq[128 + i * NFP : 128 + (i + 1) * NFP, cols] = hi
    lifted = dot(own_lift[...], xq[...])
    fresh = [state[v] - lifted[:, v * E : (v + 1) * E] for v in range(wide)]
    if thin:
        fresh = apart(fresh)
    for v in range(NV):
        base_out[v] = fresh[v] if first else jnp.where(start, fresh[v], base_ref[v])
    if first:
        thin_matrices(star, thin_star)
        thin_matrices(lflux, thin_lflux)
        thin_matrices(star, pair_star, 2)
        for u in range(NV):
            for v in range(NV):
                thin_nflux[u * NV + v : u * NV + v + 1, :] = faces_side_by_side(nflux[u, v])


def call(kernel, outs, scratch, args, raw=0):
    def memory(s):
        return pltpu.VMEM(*s) if isinstance(s, tuple) else s

    return pl.pallas_call(
        kernel,
        out_shape=[jax.ShapeDtypeStruct(s, t) for s, t in outs],
        in_specs=[pl.BlockSpec(memory_space=pltpu.HBM if n < raw else pltpu.VMEM) for n in range(len(args))],
        out_specs=[pl.BlockSpec(memory_space=pltpu.VMEM)] * len(outs),
        scratch_shapes=[memory(s) for s in scratch],
        compiler_params=pltpu.CompilerParams(vmem_limit_bytes=40 * 1024 * 1024),
    )(*args)


def body(dofs, stiffness, star, local_flux, neighbour_flux, face_proj, face_rot, cluster, neighbour, orient, send_list):
    n_dom, n_sub = lax.axis_size("dom"), lax.axis_size("sub")
    odd = lax.axis_index("dom") % 2
    chip = [(i, i ^ 1) for i in range(n_dom)]
    groups = [
        [(i + h) % n_dom * n_sub + t for h in range(2) for t in range(n_sub)] for i in range(1, n_dom, 2)
    ]
    lines = [[i * n_sub + t for t in range(n_sub)] for i in range(n_dom)]
    dom = lax.axis_index("dom")
    at_end = (dom == 0) | (dom == n_dom - 1)

    def exchange(block, among):
        return lax.all_to_all(
            block, ("dom", "sub"), split_axis=0, concat_axis=0, tiled=True, axis_index_groups=among
        )

    def across_pair(block):
        return exchange(block, groups)

    def within_line(block):
        own = exchange(jnp.where(odd == 1, block[0:4], block[4:8]), lines)
        return jnp.concatenate([own, own])

    raw = [
        send_list.reshape(1, SLOTS),
        neighbour,
        stiffness,
        jnp.transpose(face_proj, (1, 0, 2)),
        face_rot,
        cluster.reshape(1, E),
        jnp.transpose(dofs, (1, 0, 2)),
        jnp.transpose(star, (1, 2, 0, 3)),
        jnp.transpose(neighbour_flux, (1, 2, 0, 3)),
        jnp.transpose(local_flux, (1, 2, 0, 3)),
        orient,
    ]
    raw = [pltpu.with_memory_space_constraint(x, pltpu.HBM) for x in raw]
    flux_s = ((NV, NV, 4, E), F32)
    constants = [
        ((4, E), jnp.int32),
        ((1, E), jnp.int32),
        ((4, E), jnp.int32),
        ((3 * NBP, 3 * NBK), BF),
        ((4 * NFP, 3 * NBK), BF),
        ((NV, NV, 3, E), F32),
        flux_s,
        flux_s,
        ((2 * NBP, 192), BF),
        ((NBP, 192), BF),
        ((NBP, 192), BF),
        ((96, FACES), BF),
        ((16, E), jnp.int32),
    ]
    terms_s = ((ORDER, NV, NBP, E), F32)
    face_s = ((WIDE, FACES), BF)
    nsum_s = ((WIDE, FACES), F32)
    base_s = ((NV, NBP, E), F32)
    xs_s = ((3 * NBK, COLS), BF)
    xg_s = ((384, COLS), BF)
    xq_s = ((192, COLS), BF)
    sends = [terms_s, face_s, face_s, ((32, WIDE), F32), ((64, WIDE), F32)]
    fetched = [
        ((NV, NB, E), F32),
        ((3, NB, NB), F32),
        ((NF, 4, NB), F32),
        ((3, NF, NF), F32),
        ((1, SLOTS), jnp.int32),
        base_s,
        ((3 * NBP, NBK), F32),
        ((4 * NFP, NBK), F32),
        xs_s,
        pltpu.SemaphoreType.DMA((11,)),
    ]
    begun = call(
        opening,
        constants + sends,
        fetched,
        raw + [jnp.full((1, E), odd, jnp.int32)],
        raw=11,
    )
    neighbour, cluster, orient = begun[:3]
    stiff, proj, star, nflux, lflux, lift_a, lift_b, own_lift, pick, small = begun[3:13]
    terms, d_hi, d_lo, p_swap, p_rest = begun[13:]
    thin_s = ((ORDER, 3, NBP, E), F32)
    thin_columns = 3 * E
    for step in range(STEPS):
        odd_step = step % 2 == 1
        if odd_step:
            fresh, d_hi, d_lo, p_swap, p_rest = call(
                functools.partial(critical_thin, step),
                [thin_s] + sends[1:],
                [((384, thin_columns), BF), xs_s, ((3 * NBK, thin_columns), BF)],
                [came, nsum_thin, base, thin_nflux, lift_a, lift_b, small]
                + [stiff, thin_star, proj, pick, cluster, terms],
            )
        elif step > 0:
            nsum, terms, d_hi, d_lo, p_swap, p_rest = call(
                functools.partial(critical, False, step),
                [nsum_s] + sends,
                [xg_s, xs_s],
                [came, nsum, base, nflux, lift_a, lift_b, orient, small, stiff]
                + [pair_star if step % 4 == 2 else star, proj, pick, cluster, terms],
            )
        swapped = lax.ppermute(p_swap, "dom", chip)
        side = functools.partial(beside, step)
        thin_nsum_s = ((WIDE, E), F32)
        if step == 0:
            nsum, base, nsum_thin, thin_star, thin_lflux, thin_nflux, pair_star = call(
                side,
                [nsum_s, base_s, thin_nsum_s, ((21, 3, E), F32), ((21, 4, E), F32), ((NV * NV, E), F32)]
                + [((41, 3, E), F32)],
                [xs_s, xq_s],
                [terms, d_hi, d_lo, neighbour, stiff, star, proj, lflux, own_lift, cluster, small, nflux],
            )
        elif odd_step:
            nsum, base = call(
                side,
                [nsum_s, base_s],
                [((3 * NBK, thin_columns), BF), ((192, thin_columns), BF)],
                [fresh, d_hi, d_lo, neighbour, stiff, thin_star, proj, thin_lflux, own_lift, cluster]
                + [small, came, nsum, base],
            )
        else:
            nsum, base, nsum_thin = call(
                side,
                [nsum_s, base_s, thin_nsum_s],
                [xs_s, xq_s],
                [terms, d_hi, d_lo, neighbour, stiff, star, proj, lflux, own_lift, cluster, small, nsum, base],
            )
        swapped = swapped.reshape(4, H, WIDE)
        block = jnp.concatenate([p_rest.reshape(8, H, WIDE), jnp.concatenate([swapped, swapped])], axis=1)
        if odd_step:
            block, nsum, base = lax.optimization_barrier((block, nsum, base))
        else:
            block, nsum, base, nsum_thin = lax.optimization_barrier((block, nsum, base, nsum_thin))
        came = lax.cond(at_end, within_line, across_pair, block).reshape(128, WIDE)
    (out,) = call(
        functools.partial(critical, True, STEPS),
        [((NV, NB, E), F32)],
        [xg_s],
        [came, nsum, base, nflux, lift_a, lift_b, orient, small],
    )
    return jnp.transpose(out, (1, 0, 2))


def solution(mesh):
    placed = (
        P(None, None, ("dom", "sub")),
        P(),
        P(None, None, None, ("dom", "sub")),
        P(None, None, None, ("dom", "sub")),
        P(None, None, None, ("dom", "sub")),
        P(),
        P(),
        P(("dom", "sub")),
        P(None, ("dom", "sub")),
        P(None, ("dom", "sub")),
        P("dom", "sub", None),
    )
    return jax.shard_map(
        body, mesh=mesh, in_specs=placed, out_specs=P(None, None, ("dom", "sub")), check_vma=False
    )
```

```python
import functools

import jax
import jax.numpy as jnp
from jax import lax
from jax.experimental import pallas as pl
from jax.experimental.pallas import tpu as pltpu
from jax.sharding import PartitionSpec as P

ORDER = 5
STEPS = 8
NB = 35
NBP = 40
NBK = 48
NF = 15
NFP = 16
NV = 9
E = 128
H = 8
SLOTS = 96
FACES = 4 * E
WIDE = NV * NFP
COLS = NV * E
FACT = [1.0, 1.0, 2.0, 6.0, 24.0, 120.0, 720.0]
BF = jnp.bfloat16
F32 = jnp.float32


def halves(x):
    hi = x.astype(BF)
    lo = (x - hi.astype(F32)).astype(BF)
    return hi, lo


def dot(a, b):
    return jnp.dot(a, b, preferred_element_type=F32)


def fill_basis(xs_ref, values):
    pad = jnp.zeros((NBK - NBP, E), F32)
    for v in range(len(values)):
        hi, lo = halves(jnp.concatenate([values[v], pad], axis=0))
        cols = slice(v * E, (v + 1) * E)
        xs_ref[0:NBK, cols] = hi
        xs_ref[NBK : 2 * NBK, cols] = lo
        xs_ref[2 * NBK : 3 * NBK, cols] = hi


def derive(values, stiff_ref, star_ref, xs_ref):
    fill_basis(xs_ref, values)
    stiff = stiff_ref[...]
    chunks = [range(0, 4), range(4, 8), range(8, 9)]
    applied = [dot(stiff, xs_ref[:, c[0] * E : (c[-1] + 1) * E]) for c in chunks]
    acc = [None] * NV
    for chunk, piece in zip(chunks, applied):
        for d in range(3):
            for n, u in enumerate(chunk):
                part = piece[d * NBP : (d + 1) * NBP, n * E : (n + 1) * E]
                for v in range(NV):
                    term = part * star_ref[u, v, d : d + 1, :]
                    acc[v] = term if acc[v] is None else acc[v] + term
    return acc


def gather(got_ref, row_codes):
    got = jnp.concatenate(halves(got_ref[...]), axis=0)
    rows = lax.broadcasted_iota(jnp.int32, (128, E), 0)
    far = jnp.concatenate([(rows == row).astype(F32).astype(BF) for row in row_codes], axis=1)
    far = jnp.concatenate([far, far], axis=0)
    return lax.dot_general(got, far, (((0,), (0,)), ((), ())), preferred_element_type=F32)


def lane_group(shape, g=4):
    return lax.broadcasted_iota(jnp.int32, shape, len(shape) - 1) // (E // g)


def shifted(x, groups, g=4):
    return x if groups % g == 0 else pltpu.roll(x, groups % g * (E // g), x.ndim - 1)


def side_by_side(values, g=4):
    group = lane_group(values[0].shape, g)
    parts = []
    for j in range(-(-NV // g)):
        part = jnp.zeros_like(values[0])
        for n in range(min(g, NV - g * j)):
            part = jnp.where(group == n, shifted(values[g * j + n], n, g), part)
        parts.append(part)
    return parts


def apart(parts, g=4):
    return [shifted(parts[v // g], -(v % g), g) for v in range(NV)]


def over_groups(x, g):
    for distance in (1, 2)[: g // 2]:
        x = x + shifted(x, distance, g)
    return x


def faces_side_by_side(rows):
    group = lane_group((1, E))
    joined = rows[0:1, :]
    for i in range(1, 4):
        joined = jnp.where(group == i, shifted(rows[i : i + 1, :], i), joined)
    return joined


def thin_matrices(full_ref, thin_ref, g=4):
    whole = NV // g
    picks = []
    for to in range(whole):
        for of in range(whole):
            for r in range(g):
                picks.append([(g * of + (n - r) % g, g * to + n) for n in range(g)])
    picks += [[(NV - 1, g * to + n) for n in range(g)] for to in range(whole)]
    picks += [[(g * of + n, NV - 1) for n in range(g)] for of in range(whole)]
    picks.append([(NV - 1, NV - 1)])
    depth = full_ref.shape[2]
    group = lane_group((depth, E), g)
    for k, sources in enumerate(picks):
        row = jnp.zeros((depth, E), F32)
        for n, (u, v) in enumerate(sources):
            row = jnp.where(group == n, shifted(full_ref[u, v], n, g), row)
        thin_ref[k] = row


def mix(acc, parts, thin_ref, d, g=4):
    whole = NV // g
    spread = over_groups(parts[whole], g)
    terms = [[] for _ in range(whole)]
    for of in range(whole):
        for r in range(g):
            part = shifted(parts[of], r, g)
            for to in range(whole):
                terms[to].append(part * thin_ref[(to * whole + of) * g + r, d : d + 1, :])
    base = whole * whole * g
    for to in range(whole):
        terms[to].append(spread * thin_ref[base + to, d : d + 1, :])
    base = base + whole
    terms.append([part * thin_ref[base + n, d : d + 1, :] for n, part in enumerate(parts)])
    for to in range(whole + 1):
        for term in terms[to]:
            acc[to] = term if acc[to] is None else acc[to] + term


def mixed_parts(acc, g=4):
    last = over_groups(acc[-1], g)
    return acc[:-1] + [jnp.where(lane_group(last.shape, g) == 0, last, 0.0)]


def derive_thin(parts, stiff_ref, thin_ref, xt_ref, g=4):
    fill_basis(xt_ref, parts)
    applied = dot(stiff_ref[...], xt_ref[:, 0 : len(parts) * E])
    acc = [None] * len(parts)
    for d in range(3):
        rows = applied[d * NBP : (d + 1) * NBP]
        mix(acc, [rows[:, j * E : (j + 1) * E] for j in range(len(parts))], thin_ref, d, g)
    return mixed_parts(acc, g)


def weight_rows(cluster_ref, step):
    period = jnp.left_shift(jnp.int32(1), cluster_ref[...])
    offset = jnp.bitwise_and(jnp.int32(step), period - 1)
    a, inverse = offset.astype(F32), 1.0 / period.astype(F32)
    low, high, scale, rows = jnp.ones_like(a), jnp.ones_like(a), jnp.ones_like(a), []
    for k in range(ORDER):
        low, high = low * a, high * (a + 1.0)
        rows.append((high - low) * scale * (1.0 / FACT[k + 1]))
        scale = scale * inverse
    return rows, offset == 0


def expand_thin(step, current, cluster, stiff, thin, proj, pick, terms_in, terms, faced, pay_swap, pay_rest, xs, xt):
    rows, start = weight_rows(cluster, step)
    fresh = [None] * 3
    for k in range(ORDER):
        if k > 0:
            current = derive_thin(current, stiff, thin, xt)
        for j in range(3):
            terms[k, j] = current[j]
            part = current[j] * (1.0 / FACT[k + 1])
            fresh[j] = part if k == 0 else fresh[j] + part
    fresh = apart(fresh)
    total = []
    for v in range(NV):
        kept = terms_in[0, v] * rows[0]
        for k in range(1, ORDER):
            kept = kept + terms_in[k, v] * rows[k]
        total.append(jnp.where(start, fresh[v], kept))
    send(total, proj, pick, faced, pay_swap, pay_rest, xs)


def expand(step, first, upd, cluster, stiff, star, proj, pick, terms_in, terms, faced, pay_swap, pay_rest, xs):
    rows, start = weight_rows(cluster, step)
    paired = step % 4 == 2
    current = upd
    total = [None] * NV
    for k in range(ORDER):
        if paired:
            parts = side_by_side(upd, 2) if k == 0 else derive_thin(parts, stiff, star, xs, 2)
            current = upd if k == 0 else apart(parts, 2)
        elif k > 0:
            current = derive(current, stiff, star, xs)
        for v in range(NV):
            kept = current[v] if first else jnp.where(start, current[v], terms_in[k, v])
            terms[k, v] = kept
            part = kept * rows[k]
            total[v] = part if k == 0 else total[v] + part
    send(total, proj, pick, faced, pay_swap, pay_rest, xs)


def send(total, proj, pick, faced, pay_swap, pay_rest, xs):
    fill_basis(xs, total)
    faces = dot(proj[...], xs[...])
    for i in range(4):
        for v in range(NV):
            hi, lo = halves(faces[i * NFP : (i + 1) * NFP, v * E : (v + 1) * E])
            faced[v * NFP : (v + 1) * NFP, i * E : (i + 1) * E] = hi
            faced[WIDE + v * NFP : WIDE + (v + 1) * NFP, i * E : (i + 1) * E] = lo
    dims = (((1,), (1,)), ((), ()))
    pay = lax.dot_general(pick[...], faced[0:WIDE, :], dims, preferred_element_type=F32)
    pay = pay + lax.dot_general(pick[...], faced[WIDE : 2 * WIDE, :], dims, preferred_element_type=F32)
    pay_swap[...] = pay[0:32]
    pay_rest[...] = pay[32:96]


def opening(*refs):
    raw, refs = refs[:11], list(refs[11:])
    take = lambda n: [refs.pop(0) for _ in range(n)]
    odd_ref = refs.pop(0)
    neighbour_ref, cluster, orient = take(3)
    stiff, proj, star, nflux, lflux, lift_a, lift_b, own_lift, pick, small = take(10)
    terms, faced, pay_swap, pay_rest = take(4)
    dofs_s, stiff_s, proj_s, rot_s, send_ref, state, wide_s, tall_s, xs, sems = take(10)
    targets = [send_ref, neighbour_ref, stiff_s, proj_s, rot_s, cluster, dofs_s, star, nflux, lflux, orient]
    copies = [pltpu.make_async_copy(raw[n], targets[n], sems.at[n]) for n in range(11)]
    for copy in copies:
        copy.start()
    for copy in copies[:2]:
        copy.wait()

    high = lax.Precision.HIGHEST
    columns_first = (((0,), (0,)), ((), ()))

    def grid(shape):
        return lax.broadcasted_iota(jnp.int32, shape, 0), lax.broadcasted_iota(jnp.int32, shape, 1)

    odd = odd_ref[...]
    codes = neighbour_ref[...]
    slot = jnp.right_shift(codes - FACES, 2)
    block, source, place = slot >> 5, jnp.bitwise_and(slot >> 3, 3), jnp.bitwise_and(slot, 7)
    same, cross = 4 * (1 - odd), 4 * odd
    row = jnp.where(block == 2 * (1 - odd), (cross + source) * 16 + place, (same + source) * 16 + place)
    row = jnp.where(block == 2 * odd, row + H, row)
    row = jnp.where((codes >= FACES) & (codes < FACES + 4 * SLOTS), row, -1)
    small[8:12, :] = row
    small[0:1, :] = faces_side_by_side(codes)
    small[5:6, :] = faces_side_by_side(row)
    rows, columns = grid((96, SLOTS))
    flag = odd[:, 0:1]
    rest = rows - 32
    peer, place = rest >> 3, jnp.bitwise_and(rest, 7)
    inside = jnp.where((peer >> 2) == 1 - flag, 32, 64 * flag)
    wanted = inside + jnp.bitwise_and(peer, 3) * H + place
    wanted = jnp.where(rest < 0, 64 * (1 - flag) + rows, wanted)
    chooser = (columns == wanted).astype(F32)
    listed = jnp.broadcast_to(send_ref[...].astype(F32), (8, SLOTS))
    listed = lax.dot_general(chooser, listed, (((1,), (1,)), ((), ())), precision=high, preferred_element_type=F32)
    _, columns = grid((96, FACES))
    pick[...] = (columns.astype(F32) == listed[:, 0:1]).astype(F32).astype(BF)

    for copy in copies[2:5]:
        copy.wait()
    wide_s[...] = jnp.zeros_like(wide_s)
    for d in range(3):
        wide_s[d * NBP : d * NBP + NB, 0:NB] = -stiff_s[d]
    rows, columns = grid((NBK, 3 * NBK))
    twice = ((columns == rows) | (columns == rows + NBK)).astype(F32).astype(BF)
    once = (columns == rows + 2 * NBK).astype(F32).astype(BF)
    hi, lo = halves(wide_s[...])
    stiff[...] = (dot(hi, twice) + dot(lo, once)).astype(BF)
    tall_s[...] = jnp.zeros_like(tall_s)
    for i in range(4):
        for f in range(NF):
            tall_s[i * NFP + f : i * NFP + f + 1, 0:NB] = proj_s[f, i : i + 1, :]
    hi, lo = halves(tall_s[...])
    proj[...] = (dot(hi, twice) + dot(lo, once)).astype(BF)
    for copy in copies[5:8]:
        copy.wait()
    state[...] = jnp.zeros_like(state)
    for v in range(NV):
        state[v, 0:NB, :] = dofs_s[v]
    upd = [state[v] for v in range(NV)]
    expand(0, True, upd, cluster, stiff, star, proj, pick, None, terms, faced, pay_swap, pay_rest, xs)

    rows, columns = grid((64, 192))
    twice = ((columns == rows) | (columns == rows + 64)).astype(F32).astype(BF)
    once = (columns == rows + 128).astype(F32).astype(BF)
    own = lax.dot_general(hi, twice, columns_first, preferred_element_type=F32)
    own = own + lax.dot_general(lo, once, columns_first, preferred_element_type=F32)
    own_lift[...] = own[0:NBP].astype(BF)
    mixed = jnp.zeros((64, 192), F32)
    to_rows, to_columns = grid((64, NF))
    from_rows, from_columns = grid((NF, 192))
    for o in range(3):
        spread = (jnp.bitwise_and(to_rows, 15) == to_columns).astype(F32)
        spread = jnp.dot(spread, rot_s[o], precision=high, preferred_element_type=F32)
        group = from_columns // 48
        placed = (from_columns - 48 * group == o * NFP + from_rows).astype(F32)
        mixed = mixed + jnp.dot(spread, placed, precision=high, preferred_element_type=F32)
    mixed = jnp.where((rows >> 4) == columns // 48, mixed, 0.0)
    lift = lax.dot_general(tall_s[...], mixed, columns_first, precision=high, preferred_element_type=F32)
    hi, lo = halves(lift[0:NBP])
    lift_a[0:NBP, :] = hi
    lift_a[NBP : 2 * NBP, :] = lo
    lift_b[...] = hi
    for copy in copies[8:]:
        copy.wait()
    for i in range(4):
        turns = jnp.where(lane_group((1, E)) == 0, orient[i : i + 1, :], 0)
        turns = turns + shifted(turns, 1)
        small[1 + i : 2 + i, :] = turns + shifted(turns, 2)


def critical(last, step, *refs):
    refs = list(refs)
    take = lambda n: [refs.pop(0) for _ in range(n)]
    got_ref, nsum_ref, base_ref, nflux, lift_a, lift_b, orient, small = take(8)
    if last:
        out_ref, xg = take(2)
    else:
        stiff, star, proj, pick, cluster, terms_in = take(6)
        nsum_out, terms, faced, pay_swap, pay_rest, xg, xs = take(7)

    total = nsum_ref[...] + gather(got_ref, [small[8 + i : 9 + i, :] for i in range(4)])
    if not last:
        nsum_out[...] = total
    masks = []
    for i in range(4):
        chosen = [(orient[i : i + 1, :] == o).astype(F32) for o in range(3)]
        masks.append([jnp.broadcast_to(mask, (NFP, E)).astype(BF) for mask in chosen])
    upd = []
    for chunk in (range(0, 4), range(4, 8), range(8, 9)):
        for i in range(4):
            acc = {}
            for u in range(NV):
                part = total[u * NFP : (u + 1) * NFP, i * E : (i + 1) * E]
                for v in chunk:
                    term = part * nflux[u, v, i : i + 1, :]
                    acc[v] = term if u == 0 else acc[v] + term
            for v in chunk:
                hi, lo = halves(acc[v])
                cols = slice(v * E, (v + 1) * E)
                for o in range(3):
                    row = (i * 3 + o) * NFP
                    xg[row : row + NFP, cols] = hi * masks[i][o]
                    xg[192 + row : 192 + row + NFP, cols] = lo * masks[i][o]
        cols = slice(chunk[0] * E, (chunk[-1] + 1) * E)
        two = dot(lift_a[...], xg[0:192, cols])
        lifted = two[0:NBP] + two[NBP : 2 * NBP] + dot(lift_b[...], xg[192:384, cols])
        upd += [base_ref[v] + lifted[:, n * E : (n + 1) * E] for n, v in enumerate(chunk)]
    if last:
        for v in range(NV):
            out_ref[v] = upd[v][0:NB]
    else:
        expand(step, False, upd, cluster, stiff, star, proj, pick, terms_in, terms, faced, pay_swap, pay_rest, xs)


def critical_thin(step, *refs):
    got_ref, nsum_ref, base_ref, nflux, lift_a, lift_b, small, stiff, star, proj, pick, cluster, terms_in = refs[:13]
    terms, faced, pay_swap, pay_rest, xg, xs, xt = refs[13:]
    total = nsum_ref[...] + gather(got_ref, [small[5:6, :]])
    acc = [None] * NV
    for u in range(NV):
        part = total[u * NFP : (u + 1) * NFP, :]
        for v in range(NV):
            term = part * nflux[u * NV + v : u * NV + v + 1, :]
            acc[v] = term if acc[v] is None else acc[v] + term
    group = lane_group((NFP, E))
    for i in range(4):
        chosen = []
        for o in range(3):
            mask = (small[1 + i : 2 + i, :] == o).astype(F32)
            chosen.append(jnp.broadcast_to(mask, (NFP, E)).astype(BF))
        for j in range(3):
            part = jnp.zeros((NFP, E), F32)
            for g in range(min(4, NV - 4 * j)):
                part = jnp.where(group == g, shifted(acc[4 * j + g], g - i), part)
            hi, lo = halves(part)
            cols = slice(j * E, (j + 1) * E)
            for o in range(3):
                row = (i * 3 + o) * NFP
                xg[row : row + NFP, cols] = hi * chosen[o]
                xg[192 + row : 192 + row + NFP, cols] = lo * chosen[o]
    two = dot(lift_a[...], xg[0:192, :])
    lifted = two[0:NBP] + two[NBP : 2 * NBP] + dot(lift_b[...], xg[192:384, :])
    base = side_by_side([base_ref[v] for v in range(NV)])
    upd = [base[j] + lifted[:, j * E : (j + 1) * E] for j in range(3)]
    expand_thin(step, upd, cluster, stiff, star, proj, pick, terms_in, terms, faced, pay_swap, pay_rest, xs, xt)


def beside(step, *refs):
    refs = list(refs)
    take = lambda n: [refs.pop(0) for _ in range(n)]
    first, thin = step == 0, step % 2 == 1
    terms, faced, neighbour, stiff, star, proj, lflux, own_lift, cluster = take(9)
    small = refs.pop(0)
    if thin:
        got_ref = refs.pop(0)
    if first:
        nflux = refs.pop(0)
    else:
        nsum_ref, base_ref = take(2)
    nsum_out, base_out = take(2)
    if not thin:
        nsum_thin = refs.pop(0)
    if first:
        thin_star, thin_lflux, thin_nflux, pair_star = take(4)
    xs, xq = take(2)
    _, start = weight_rows(cluster, step)
    period = jnp.left_shift(jnp.int32(1), cluster[...]).astype(F32)
    face_rows = lax.broadcasted_iota(jnp.int32, (FACES, E), 0)
    wanted = [neighbour[i : i + 1, :] for i in range(4)] + ([] if thin else [small[0:1, :]])
    near = jnp.concatenate([(face_rows == row).astype(F32).astype(BF) for row in wanted], axis=1)
    gathered = dot(faced[...], near)
    gathered = gathered[0:WIDE] + gathered[WIDE : 2 * WIDE]
    if thin:
        arrived = gather(got_ref, [small[8 + i : 9 + i, :] for i in range(4)])
    for i in range(4):
        cols = slice(i * E, (i + 1) * E)
        fresh = gathered[:, cols]
        if not first:
            kept = nsum_ref[:, cols]
            if thin:
                kept = kept + arrived[:, cols]
            fresh = fresh + jnp.where(start, 0.0, kept)
        nsum_out[:, cols] = fresh
    if not thin:
        nsum_thin[...] = gathered[:, FACES : FACES + E]
    wide = 3 if thin else NV
    held = [[terms[k, v] for v in range(wide)] for k in range(ORDER)]
    if thin:
        final = derive_thin(held[ORDER - 1], stiff, star, xs)
    else:
        final = derive(held[ORDER - 1], stiff, star, xs)
    state = []
    whole = []
    for v in range(wide):
        volume = final[v] * (1.0 / FACT[ORDER])
        own = held[0][v]
        for k in range(1, ORDER):
            volume = volume + held[k][v] * (1.0 / FACT[k])
            own = own + held[k][v] * (1.0 / FACT[k + 1])
        state.append(held[0][v] + volume)
        whole.append(own if thin else own * period)
    fill_basis(xs, whole)
    faces = dot(proj[...], xs[...])
    for i in range(4):
        rows = faces[i * NFP : (i + 1) * NFP]
        acc = [None] * wide
        if thin:
            mix(acc, [rows[:, j * E : (j + 1) * E] for j in range(3)], lflux, i)
            acc = mixed_parts(acc)
        else:
            for u in range(NV):
                part = rows[:, u * E : (u + 1) * E]
                for v in range(NV):
                    term = part * lflux[u, v, i : i + 1, :]
                    acc[v] = term if acc[v] is None else acc[v] + term
        for v in range(wide):
            hi, lo = halves(acc[v])
            cols = slice(v * E, (v + 1) * E)
            xq[i * NFP : (i + 1) * NFP, cols] = hi
            xq[64 + i * NFP : 64 + (i + 1) * NFP, cols] = lo
            xq[128 + i * NFP : 128 + (i + 1) * NFP, cols] = hi
    lifted = dot(own_lift[...], xq[...])
    fresh = [state[v] - lifted[:, v * E : (v + 1) * E] for v in range(wide)]
    if thin:
        fresh = apart(fresh)
    for v in range(NV):
        base_out[v] = fresh[v] if first else jnp.where(start, fresh[v], base_ref[v])
    if first:
        thin_matrices(star, thin_star)
        thin_matrices(lflux, thin_lflux)
        thin_matrices(star, pair_star, 2)
        for u in range(NV):
            for v in range(NV):
                thin_nflux[u * NV + v : u * NV + v + 1, :] = faces_side_by_side(nflux[u, v])


def call(kernel, outs, scratch, args, raw=0):
    def memory(s):
        return pltpu.VMEM(*s) if isinstance(s, tuple) else s

    return pl.pallas_call(
        kernel,
        out_shape=[jax.ShapeDtypeStruct(s, t) for s, t in outs],
        in_specs=[pl.BlockSpec(memory_space=pltpu.HBM if n < raw else pltpu.VMEM) for n in range(len(args))],
        out_specs=[pl.BlockSpec(memory_space=pltpu.VMEM)] * len(outs),
        scratch_shapes=[memory(s) for s in scratch],
        compiler_params=pltpu.CompilerParams(vmem_limit_bytes=40 * 1024 * 1024),
    )(*args)


def body(dofs, stiffness, star, local_flux, neighbour_flux, face_proj, face_rot, cluster, neighbour, orient, send_list):
    n_dom, n_sub = lax.axis_size("dom"), lax.axis_size("sub")
    odd = lax.axis_index("dom") % 2
    chip = [(i, i ^ 1) for i in range(n_dom)]
    groups = [
        [(i + h) % n_dom * n_sub + t for h in range(2) for t in range(n_sub)] for i in range(1, n_dom, 2)
    ]
    lines = [[i * n_sub + t for t in range(n_sub)] for i in range(n_dom)]
    dom = lax.axis_index("dom")
    at_end = (dom == 0) | (dom == n_dom - 1)

    def exchange(block, among):
        return lax.all_to_all(
            block, ("dom", "sub"), split_axis=0, concat_axis=0, tiled=True, axis_index_groups=among
        )

    def across_pair(block):
        return exchange(block, groups)

    def within_line(block):
        own = exchange(jnp.where(odd == 1, block[0:4], block[4:8]), lines)
        return jnp.concatenate([own, own])

    raw = [
        send_list.reshape(1, SLOTS),
        neighbour,
        stiffness,
        jnp.transpose(face_proj, (1, 0, 2)),
        face_rot,
        cluster.reshape(1, E),
        jnp.transpose(dofs, (1, 0, 2)),
        jnp.transpose(star, (1, 2, 0, 3)),
        jnp.transpose(neighbour_flux, (1, 2, 0, 3)),
        jnp.transpose(local_flux, (1, 2, 0, 3)),
        orient,
    ]
    raw = [pltpu.with_memory_space_constraint(x, pltpu.HBM) for x in raw]
    flux_s = ((NV, NV, 4, E), F32)
    constants = [
        ((4, E), jnp.int32),
        ((1, E), jnp.int32),
        ((4, E), jnp.int32),
        ((3 * NBP, 3 * NBK), BF),
        ((4 * NFP, 3 * NBK), BF),
        ((NV, NV, 3, E), F32),
        flux_s,
        flux_s,
        ((2 * NBP, 192), BF),
        ((NBP, 192), BF),
        ((NBP, 192), BF),
        ((96, FACES), BF),
        ((16, E), jnp.int32),
    ]
    terms_s = ((ORDER, NV, NBP, E), F32)
    face_s = ((2 * WIDE, FACES), BF)
    nsum_s = ((WIDE, FACES), F32)
    base_s = ((NV, NBP, E), F32)
    xs_s = ((3 * NBK, COLS), BF)
    xg_s = ((384, COLS), BF)
    xq_s = ((192, COLS), BF)
    sends = [terms_s, face_s, ((32, WIDE), F32), ((64, WIDE), F32)]
    fetched = [
        ((NV, NB, E), F32),
        ((3, NB, NB), F32),
        ((NF, 4, NB), F32),
        ((3, NF, NF), F32),
        ((1, SLOTS), jnp.int32),
        base_s,
        ((3 * NBP, NBK), F32),
        ((4 * NFP, NBK), F32),
        xs_s,
        pltpu.SemaphoreType.DMA((11,)),
    ]
    begun = call(
        opening,
        constants + sends,
        fetched,
        raw + [jnp.full((1, E), odd, jnp.int32)],
        raw=11,
    )
    neighbour, cluster, orient = begun[:3]
    stiff, proj, star, nflux, lflux, lift_a, lift_b, own_lift, pick, small = begun[3:13]
    terms, faced, p_swap, p_rest = begun[13:]
    thin_s = ((ORDER, 3, NBP, E), F32)
    thin_columns = 3 * E
    for step in range(STEPS):
        odd_step = step % 2 == 1
        if odd_step:
            fresh, faced, p_swap, p_rest = call(
                functools.partial(critical_thin, step),
                [thin_s] + sends[1:],
                [((384, thin_columns), BF), xs_s, ((3 * NBK, thin_columns), BF)],
                [came, nsum_thin, base, thin_nflux, lift_a, lift_b, small]
                + [stiff, thin_star, proj, pick, cluster, terms],
            )
        elif step > 0:
            nsum, terms, faced, p_swap, p_rest = call(
                functools.partial(critical, False, step),
                [nsum_s] + sends,
                [xg_s, xs_s],
                [came, nsum, base, nflux, lift_a, lift_b, orient, small, stiff]
                + [pair_star if step % 4 == 2 else star, proj, pick, cluster, terms],
            )
        swapped = lax.ppermute(p_swap, "dom", chip)
        side = functools.partial(beside, step)
        thin_nsum_s = ((WIDE, E), F32)
        if step == 0:
            nsum, base, nsum_thin, thin_star, thin_lflux, thin_nflux, pair_star = call(
                side,
                [nsum_s, base_s, thin_nsum_s, ((21, 3, E), F32), ((21, 4, E), F32), ((NV * NV, E), F32)]
                + [((41, 3, E), F32)],
                [xs_s, xq_s],
                [terms, faced, neighbour, stiff, star, proj, lflux, own_lift, cluster, small, nflux],
            )
        elif odd_step:
            nsum, base = call(
                side,
                [nsum_s, base_s],
                [((3 * NBK, thin_columns), BF), ((192, thin_columns), BF)],
                [fresh, faced, neighbour, stiff, thin_star, proj, thin_lflux, own_lift, cluster]
                + [small, came, nsum, base],
            )
        else:
            nsum, base, nsum_thin = call(
                side,
                [nsum_s, base_s, thin_nsum_s],
                [xs_s, xq_s],
                [terms, faced, neighbour, stiff, star, proj, lflux, own_lift, cluster, small, nsum, base],
            )
        swapped = swapped.reshape(4, H, WIDE)
        block = jnp.concatenate([p_rest.reshape(8, H, WIDE), jnp.concatenate([swapped, swapped])], axis=1)
        if odd_step:
            block, nsum, base = lax.optimization_barrier((block, nsum, base))
        else:
            block, nsum, base, nsum_thin = lax.optimization_barrier((block, nsum, base, nsum_thin))
        came = lax.cond(at_end, within_line, across_pair, block).reshape(128, WIDE)
    (out,) = call(
        functools.partial(critical, True, STEPS),
        [((NV, NB, E), F32)],
        [xg_s],
        [came, nsum, base, nflux, lift_a, lift_b, orient, small],
    )
    return jnp.transpose(out, (1, 0, 2))


def solution(mesh):
    placed = (
        P(None, None, ("dom", "sub")),
        P(),
        P(None, None, None, ("dom", "sub")),
        P(None, None, None, ("dom", "sub")),
        P(None, None, None, ("dom", "sub")),
        P(),
        P(),
        P(("dom", "sub")),
        P(None, ("dom", "sub")),
        P(None, ("dom", "sub")),
        P("dom", "sub", None),
    )
    return jax.shard_map(
        body, mesh=mesh, in_specs=placed, out_specs=P(None, None, ("dom", "sub")), check_vma=False
    )
```

```python
import functools

import jax
import jax.numpy as jnp
from jax import lax
from jax.experimental import pallas as pl
from jax.experimental.pallas import tpu as pltpu
from jax.sharding import PartitionSpec as P

ORDER = 5
STEPS = 8
NB = 35
NBP = 40
NBK = 48
NF = 15
NFP = 16
NV = 9
E = 128
H = 8
SLOTS = 96
FACES = 4 * E
WIDE = NV * NFP
COLS = NV * E
FACT = [1.0, 1.0, 2.0, 6.0, 24.0, 120.0, 720.0]
BF = jnp.bfloat16
F32 = jnp.float32


def halves(x):
    hi = x.astype(BF)
    lo = (x - hi.astype(F32)).astype(BF)
    return hi, lo


def dot(a, b):
    return jnp.dot(a, b, preferred_element_type=F32)


def fill_basis(xs_ref, values):
    pad = jnp.zeros((NBK - NBP, E), F32)
    for v in range(len(values)):
        hi, lo = halves(jnp.concatenate([values[v], pad], axis=0))
        cols = slice(v * E, (v + 1) * E)
        xs_ref[0:NBK, cols] = hi
        xs_ref[NBK : 2 * NBK, cols] = lo
        xs_ref[2 * NBK : 3 * NBK, cols] = hi


def derive(values, stiff_ref, star_ref, xs_ref):
    fill_basis(xs_ref, values)
    stiff = stiff_ref[...]
    chunks = [range(0, 4), range(4, 8), range(8, 9)]
    applied = [dot(stiff, xs_ref[:, c[0] * E : (c[-1] + 1) * E]) for c in chunks]
    acc = [None] * NV
    for chunk, piece in zip(chunks, applied):
        for d in range(3):
            for n, u in enumerate(chunk):
                part = piece[d * NBP : (d + 1) * NBP, n * E : (n + 1) * E]
                for v in range(NV):
                    term = part * star_ref[u, v, d : d + 1, :]
                    acc[v] = term if acc[v] is None else acc[v] + term
    return acc


def gather(got_ref, row_codes):
    got = jnp.concatenate(halves(got_ref[...]), axis=0)
    rows = lax.broadcasted_iota(jnp.int32, (128, E), 0)
    far = jnp.concatenate([(rows == row).astype(F32).astype(BF) for row in row_codes], axis=1)
    far = jnp.concatenate([far, far], axis=0)
    return lax.dot_general(got, far, (((0,), (0,)), ((), ())), preferred_element_type=F32)


def lane_group(shape, g=4):
    return lax.broadcasted_iota(jnp.int32, shape, len(shape) - 1) // (E // g)


def shifted(x, groups, g=4):
    return x if groups % g == 0 else pltpu.roll(x, groups % g * (E // g), x.ndim - 1)


def side_by_side(values, g=4):
    group = lane_group(values[0].shape, g)
    parts = []
    for j in range(-(-NV // g)):
        part = jnp.zeros_like(values[0])
        for n in range(min(g, NV - g * j)):
            part = jnp.where(group == n, shifted(values[g * j + n], n, g), part)
        parts.append(part)
    return parts


def apart(parts, g=4):
    return [shifted(parts[v // g], -(v % g), g) for v in range(NV)]


def over_groups(x, g):
    for distance in (1, 2)[: g // 2]:
        x = x + shifted(x, distance, g)
    return x


def faces_side_by_side(rows):
    group = lane_group((1, E))
    joined = rows[0:1, :]
    for i in range(1, 4):
        joined = jnp.where(group == i, shifted(rows[i : i + 1, :], i), joined)
    return joined


def thin_matrices(full_ref, thin_ref, g=4):
    whole = NV // g
    picks = []
    for to in range(whole):
        for of in range(whole):
            for r in range(g):
                picks.append([(g * of + (n - r) % g, g * to + n) for n in range(g)])
    picks += [[(NV - 1, g * to + n) for n in range(g)] for to in range(whole)]
    picks += [[(g * of + n, NV - 1) for n in range(g)] for of in range(whole)]
    picks.append([(NV - 1, NV - 1)])
    depth = full_ref.shape[2]
    group = lane_group((depth, E), g)
    for k, sources in enumerate(picks):
        row = jnp.zeros((depth, E), F32)
        for n, (u, v) in enumerate(sources):
            row = jnp.where(group == n, shifted(full_ref[u, v], n, g), row)
        thin_ref[k] = row


def mix(acc, parts, thin_ref, d, g=4):
    whole = NV // g
    spread = over_groups(parts[whole], g)
    terms = [[] for _ in range(whole)]
    for of in range(whole):
        for r in range(g):
            part = shifted(parts[of], r, g)
            for to in range(whole):
                terms[to].append(part * thin_ref[(to * whole + of) * g + r, d : d + 1, :])
    base = whole * whole * g
    for to in range(whole):
        terms[to].append(spread * thin_ref[base + to, d : d + 1, :])
    base = base + whole
    terms.append([part * thin_ref[base + n, d : d + 1, :] for n, part in enumerate(parts)])
    for to in range(whole + 1):
        for term in terms[to]:
            acc[to] = term if acc[to] is None else acc[to] + term


def mixed_parts(acc, g=4):
    last = over_groups(acc[-1], g)
    return acc[:-1] + [jnp.where(lane_group(last.shape, g) == 0, last, 0.0)]


def derive_thin(parts, stiff_ref, thin_ref, xt_ref, g=4):
    fill_basis(xt_ref, parts)
    applied = dot(stiff_ref[...], xt_ref[:, 0 : len(parts) * E])
    acc = [None] * len(parts)
    for d in range(3):
        rows = applied[d * NBP : (d + 1) * NBP]
        mix(acc, [rows[:, j * E : (j + 1) * E] for j in range(len(parts))], thin_ref, d, g)
    return mixed_parts(acc, g)


def weight_rows(cluster_ref, step):
    period = jnp.left_shift(jnp.int32(1), cluster_ref[...])
    offset = jnp.bitwise_and(jnp.int32(step), period - 1)
    a, inverse = offset.astype(F32), 1.0 / period.astype(F32)
    low, high, scale, rows = jnp.ones_like(a), jnp.ones_like(a), jnp.ones_like(a), []
    for k in range(ORDER):
        low, high = low * a, high * (a + 1.0)
        rows.append((high - low) * scale * (1.0 / FACT[k + 1]))
        scale = scale * inverse
    return rows, offset == 0


def expand_thin(step, current, cluster, stiff, thin, proj, pick, terms_in, terms, faced, pay_swap, pay_rest, xs, xt):
    rows, start = weight_rows(cluster, step)
    fresh = [None] * 3
    for k in range(ORDER):
        if k > 0:
            current = derive_thin(current, stiff, thin, xt)
        for j in range(3):
            terms[k, j] = current[j]
            part = current[j] * (1.0 / FACT[k + 1])
            fresh[j] = part if k == 0 else fresh[j] + part
    fresh = apart(fresh)
    total = []
    for v in range(NV):
        kept = terms_in[0, v] * rows[0]
        for k in range(1, ORDER):
            kept = kept + terms_in[k, v] * rows[k]
        total.append(jnp.where(start, fresh[v], kept))
    send(total, proj, pick, faced, pay_swap, pay_rest, xs)


def expand(step, first, upd, cluster, stiff, star, proj, pick, terms_in, terms, faced, pay_swap, pay_rest, xs):
    rows, start = weight_rows(cluster, step)
    paired = step % 4 == 2
    current = upd
    total = [None] * NV
    for k in range(ORDER):
        if paired:
            parts = side_by_side(upd, 2) if k == 0 else derive_thin(parts, stiff, star, xs, 2)
            current = upd if k == 0 else apart(parts, 2)
        elif k > 0:
            current = derive(current, stiff, star, xs)
        for v in range(NV):
            kept = current[v] if first else jnp.where(start, current[v], terms_in[k, v])
            terms[k, v] = kept
            part = kept * rows[k]
            total[v] = part if k == 0 else total[v] + part
    send(total, proj, pick, faced, pay_swap, pay_rest, xs)


def send(total, proj, pick, faced, pay_swap, pay_rest, xs):
    fill_basis(xs, total)
    faces = dot(proj[...], xs[...])
    for i in range(4):
        for v in range(NV):
            hi, lo = halves(faces[i * NFP : (i + 1) * NFP, v * E : (v + 1) * E])
            faced[v * NFP : (v + 1) * NFP, i * E : (i + 1) * E] = hi
            faced[WIDE + v * NFP : WIDE + (v + 1) * NFP, i * E : (i + 1) * E] = lo
    dims = (((1,), (1,)), ((), ()))
    pay = lax.dot_general(pick[...], faced[0:WIDE, :], dims, preferred_element_type=F32)
    pay = pay + lax.dot_general(pick[...], faced[WIDE : 2 * WIDE, :], dims, preferred_element_type=F32)
    pay_swap[...] = pay[0:32]
    pay_rest[...] = pay[32:96]


def opening(*refs):
    raw, refs = refs[:11], list(refs[11:])
    take = lambda n: [refs.pop(0) for _ in range(n)]
    odd_ref = refs.pop(0)
    neighbour_ref, cluster, orient = take(3)
    stiff, proj, star, nflux, lflux, lift_a, lift_b, own_lift, pick, small = take(10)
    terms, faced, pay_swap, pay_rest = take(4)
    dofs_s, stiff_s, proj_s, rot_s, send_ref, state, wide_s, tall_s, xs, sems = take(10)
    targets = [send_ref, neighbour_ref, stiff_s, proj_s, rot_s, cluster, dofs_s, star, nflux, lflux, orient]
    copies = [pltpu.make_async_copy(raw[n], targets[n], sems.at[n]) for n in range(11)]
    for copy in copies:
        copy.start()
    for copy in copies[:2]:
        copy.wait()

    high = lax.Precision.HIGHEST
    columns_first = (((0,), (0,)), ((), ()))

    def grid(shape):
        return lax.broadcasted_iota(jnp.int32, shape, 0), lax.broadcasted_iota(jnp.int32, shape, 1)

    odd = odd_ref[...]
    codes = neighbour_ref[...]
    slot = jnp.right_shift(codes - FACES, 2)
    block, source, place = slot >> 5, jnp.bitwise_and(slot >> 3, 3), jnp.bitwise_and(slot, 7)
    same, cross = 4 * (1 - odd), 4 * odd
    row = jnp.where(block == 2 * (1 - odd), (cross + source) * 16 + place, (same + source) * 16 + place)
    row = jnp.where(block == 2 * odd, row + H, row)
    row = jnp.where((codes >= FACES) & (codes < FACES + 4 * SLOTS), row, -1)
    small[8:12, :] = row
    small[0:1, :] = faces_side_by_side(codes)
    small[5:6, :] = faces_side_by_side(row)
    rows, columns = grid((96, SLOTS))
    flag = odd[:, 0:1]
    rest = rows - 32
    peer, place = rest >> 3, jnp.bitwise_and(rest, 7)
    inside = jnp.where((peer >> 2) == 1 - flag, 32, 64 * flag)
    wanted = inside + jnp.bitwise_and(peer, 3) * H + place
    wanted = jnp.where(rest < 0, 64 * (1 - flag) + rows, wanted)
    chooser = (columns == wanted).astype(F32)
    listed = jnp.broadcast_to(send_ref[...].astype(F32), (8, SLOTS))
    listed = lax.dot_general(chooser, listed, (((1,), (1,)), ((), ())), precision=high, preferred_element_type=F32)
    _, columns = grid((96, FACES))
    pick[...] = (columns.astype(F32) == listed[:, 0:1]).astype(F32).astype(BF)

    for copy in copies[2:5]:
        copy.wait()
    wide_s[...] = jnp.zeros_like(wide_s)
    for d in range(3):
        wide_s[d * NBP : d * NBP + NB, 0:NB] = -stiff_s[d]
    rows, columns = grid((NBK, 3 * NBK))
    twice = ((columns == rows) | (columns == rows + NBK)).astype(F32).astype(BF)
    once = (columns == rows + 2 * NBK).astype(F32).astype(BF)
    hi, lo = halves(wide_s[...])
    stiff[...] = (dot(hi, twice) + dot(lo, once)).astype(BF)
    tall_s[...] = jnp.zeros_like(tall_s)
    for i in range(4):
        for f in range(NF):
            tall_s[i * NFP + f : i * NFP + f + 1, 0:NB] = proj_s[f, i : i + 1, :]
    hi, lo = halves(tall_s[...])
    proj[...] = (dot(hi, twice) + dot(lo, once)).astype(BF)
    for copy in copies[5:8]:
        copy.wait()
    state[...] = jnp.zeros_like(state)
    for v in range(NV):
        state[v, 0:NB, :] = dofs_s[v]
    upd = [state[v] for v in range(NV)]
    expand(0, True, upd, cluster, stiff, star, proj, pick, None, terms, faced, pay_swap, pay_rest, xs)

    rows, columns = grid((64, 192))
    twice = ((columns == rows) | (columns == rows + 64)).astype(F32).astype(BF)
    once = (columns == rows + 128).astype(F32).astype(BF)
    own = lax.dot_general(hi, twice, columns_first, preferred_element_type=F32)
    own = own + lax.dot_general(lo, once, columns_first, preferred_element_type=F32)
    own_lift[...] = own[0:NBP].astype(BF)
    mixed = jnp.zeros((64, 192), F32)
    to_rows, to_columns = grid((64, NF))
    from_rows, from_columns = grid((NF, 192))
    for o in range(3):
        spread = (jnp.bitwise_and(to_rows, 15) == to_columns).astype(F32)
        spread = jnp.dot(spread, rot_s[o], precision=high, preferred_element_type=F32)
        group = from_columns // 48
        placed = (from_columns - 48 * group == o * NFP + from_rows).astype(F32)
        mixed = mixed + jnp.dot(spread, placed, precision=high, preferred_element_type=F32)
    mixed = jnp.where((rows >> 4) == columns // 48, mixed, 0.0)
    lift = lax.dot_general(tall_s[...], mixed, columns_first, precision=high, preferred_element_type=F32)
    hi, lo = halves(lift[0:NBP])
    lift_a[0:NBP, :] = hi
    lift_a[NBP : 2 * NBP, :] = lo
    lift_b[...] = hi
    for copy in copies[8:]:
        copy.wait()
    for i in range(4):
        turns = jnp.where(lane_group((1, E)) == 0, orient[i : i + 1, :], 0)
        turns = turns + shifted(turns, 1)
        small[1 + i : 2 + i, :] = turns + shifted(turns, 2)


def critical(last, step, *refs):
    refs = list(refs)
    take = lambda n: [refs.pop(0) for _ in range(n)]
    got_ref, nsum_ref, base_ref, nflux, lift_a, lift_b, orient, small = take(8)
    if last:
        out_ref, xg = take(2)
    else:
        stiff, star, proj, pick, cluster, terms_in = take(6)
        nsum_out, terms, faced, pay_swap, pay_rest, xg, xs = take(7)

    total = nsum_ref[...] + gather(got_ref, [small[8 + i : 9 + i, :] for i in range(4)])
    if not last:
        nsum_out[...] = total
    masks = []
    for i in range(4):
        chosen = [(orient[i : i + 1, :] == o).astype(F32) for o in range(3)]
        masks.append([jnp.broadcast_to(mask, (NFP, E)).astype(BF) for mask in chosen])
    upd = []
    for chunk in (range(0, 4), range(4, 8), range(8, 9)):
        for i in range(4):
            acc = {}
            for u in range(NV):
                part = total[u * NFP : (u + 1) * NFP, i * E : (i + 1) * E]
                for v in chunk:
                    term = part * nflux[u, v, i : i + 1, :]
                    acc[v] = term if u == 0 else acc[v] + term
            for v in chunk:
                hi, lo = halves(acc[v])
                cols = slice(v * E, (v + 1) * E)
                for o in range(3):
                    row = (i * 3 + o) * NFP
                    xg[row : row + NFP, cols] = hi * masks[i][o]
                    xg[192 + row : 192 + row + NFP, cols] = lo * masks[i][o]
        cols = slice(chunk[0] * E, (chunk[-1] + 1) * E)
        two = dot(lift_a[...], xg[0:192, cols])
        lifted = two[0:NBP] + two[NBP : 2 * NBP] + dot(lift_b[...], xg[192:384, cols])
        upd += [base_ref[v] + lifted[:, n * E : (n + 1) * E] for n, v in enumerate(chunk)]
    if last:
        for v in range(NV):
            out_ref[v] = upd[v][0:NB]
    else:
        expand(step, False, upd, cluster, stiff, star, proj, pick, terms_in, terms, faced, pay_swap, pay_rest, xs)


def critical_thin(step, *refs):
    got_ref, nsum_ref, base_ref, nflux, lift_a, lift_b, small, stiff, star, proj, pick, cluster, terms_in = refs[:13]
    terms, faced, pay_swap, pay_rest, xg, xs, xt = refs[13:]
    total = nsum_ref[...] + gather(got_ref, [small[5:6, :]])
    acc = [None] * NV
    for u in range(NV):
        part = total[u * NFP : (u + 1) * NFP, :]
        for v in range(NV):
            term = part * nflux[u * NV + v : u * NV + v + 1, :]
            acc[v] = term if acc[v] is None else acc[v] + term
    group = lane_group((NFP, E))
    for i in range(4):
        chosen = []
        for o in range(3):
            mask = (small[1 + i : 2 + i, :] == o).astype(F32)
            chosen.append(jnp.broadcast_to(mask, (NFP, E)).astype(BF))
        for j in range(3):
            part = jnp.zeros((NFP, E), F32)
            for g in range(min(4, NV - 4 * j)):
                part = jnp.where(group == g, shifted(acc[4 * j + g], g - i), part)
            hi, lo = halves(part)
            cols = slice(j * E, (j + 1) * E)
            for o in range(3):
                row = (i * 3 + o) * NFP
                xg[row : row + NFP, cols] = hi * chosen[o]
                xg[192 + row : 192 + row + NFP, cols] = lo * chosen[o]
    two = dot(lift_a[...], xg[0:192, :])
    lifted = two[0:NBP] + two[NBP : 2 * NBP] + dot(lift_b[...], xg[192:384, :])
    base = side_by_side([base_ref[v] for v in range(NV)])
    upd = [base[j] + lifted[:, j * E : (j + 1) * E] for j in range(3)]
    expand_thin(step, upd, cluster, stiff, star, proj, pick, terms_in, terms, faced, pay_swap, pay_rest, xs, xt)


def beside(step, *refs):
    refs = list(refs)
    take = lambda n: [refs.pop(0) for _ in range(n)]
    first, thin = step == 0, step % 2 == 1
    terms, faced, neighbour, stiff, star, proj, lflux, own_lift, cluster = take(9)
    small = refs.pop(0)
    if thin:
        got_ref = refs.pop(0)
    if first:
        nflux = refs.pop(0)
    else:
        nsum_ref, base_ref = take(2)
    nsum_out, base_out = take(2)
    if not thin:
        nsum_thin = refs.pop(0)
    if first:
        thin_star, thin_lflux, thin_nflux, pair_star = take(4)
    xs, xq = take(2)
    _, start = weight_rows(cluster, step)
    period = jnp.left_shift(jnp.int32(1), cluster[...]).astype(F32)
    face_rows = lax.broadcasted_iota(jnp.int32, (FACES, E), 0)
    wanted = [neighbour[i : i + 1, :] for i in range(4)] + ([] if thin else [small[0:1, :]])
    near = jnp.concatenate([(face_rows == row).astype(F32).astype(BF) for row in wanted], axis=1)
    gathered = dot(faced[...], near)
    gathered = gathered[0:WIDE] + gathered[WIDE : 2 * WIDE]
    if thin:
        arrived = gather(got_ref, [small[8 + i : 9 + i, :] for i in range(4)])
    for i in range(4):
        cols = slice(i * E, (i + 1) * E)
        fresh = gathered[:, cols]
        if not first:
            kept = nsum_ref[:, cols]
            if thin:
                kept = kept + arrived[:, cols]
            fresh = fresh + jnp.where(start, 0.0, kept)
        nsum_out[:, cols] = fresh
    if not thin:
        nsum_thin[...] = gathered[:, FACES : FACES + E]
    wide = 3 if thin else NV
    held = [[terms[k, v] for v in range(wide)] for k in range(ORDER)]
    if thin:
        final = derive_thin(held[ORDER - 1], stiff, star, xs)
    elif step % 4 == 2:
        final = apart(derive_thin(side_by_side(held[ORDER - 1], 2), stiff, star, xs, 2), 2)
    else:
        final = derive(held[ORDER - 1], stiff, star, xs)
    state = []
    whole = []
    for v in range(wide):
        volume = final[v] * (1.0 / FACT[ORDER])
        own = held[0][v]
        for k in range(1, ORDER):
            volume = volume + held[k][v] * (1.0 / FACT[k])
            own = own + held[k][v] * (1.0 / FACT[k + 1])
        state.append(held[0][v] + volume)
        whole.append(own if thin else own * period)
    fill_basis(xs, whole)
    faces = dot(proj[...], xs[...])
    for i in range(4):
        rows = faces[i * NFP : (i + 1) * NFP]
        acc = [None] * wide
        if thin:
            mix(acc, [rows[:, j * E : (j + 1) * E] for j in range(3)], lflux, i)
            acc = mixed_parts(acc)
        else:
            for u in range(NV):
                part = rows[:, u * E : (u + 1) * E]
                for v in range(NV):
                    term = part * lflux[u, v, i : i + 1, :]
                    acc[v] = term if acc[v] is None else acc[v] + term
        for v in range(wide):
            hi, lo = halves(acc[v])
            cols = slice(v * E, (v + 1) * E)
            xq[i * NFP : (i + 1) * NFP, cols] = hi
            xq[64 + i * NFP : 64 + (i + 1) * NFP, cols] = lo
            xq[128 + i * NFP : 128 + (i + 1) * NFP, cols] = hi
    lifted = dot(own_lift[...], xq[...])
    fresh = [state[v] - lifted[:, v * E : (v + 1) * E] for v in range(wide)]
    if thin:
        fresh = apart(fresh)
    for v in range(NV):
        base_out[v] = fresh[v] if first else jnp.where(start, fresh[v], base_ref[v])
    if first:
        thin_matrices(star, thin_star)
        thin_matrices(lflux, thin_lflux)
        thin_matrices(star, pair_star, 2)
        for u in range(NV):
            for v in range(NV):
                thin_nflux[u * NV + v : u * NV + v + 1, :] = faces_side_by_side(nflux[u, v])


def call(kernel, outs, scratch, args, raw=0):
    def memory(s):
        return pltpu.VMEM(*s) if isinstance(s, tuple) else s

    return pl.pallas_call(
        kernel,
        out_shape=[jax.ShapeDtypeStruct(s, t) for s, t in outs],
        in_specs=[pl.BlockSpec(memory_space=pltpu.HBM if n < raw else pltpu.VMEM) for n in range(len(args))],
        out_specs=[pl.BlockSpec(memory_space=pltpu.VMEM)] * len(outs),
        scratch_shapes=[memory(s) for s in scratch],
        compiler_params=pltpu.CompilerParams(vmem_limit_bytes=40 * 1024 * 1024),
    )(*args)


def body(dofs, stiffness, star, local_flux, neighbour_flux, face_proj, face_rot, cluster, neighbour, orient, send_list):
    n_dom, n_sub = lax.axis_size("dom"), lax.axis_size("sub")
    odd = lax.axis_index("dom") % 2
    chip = [(i, i ^ 1) for i in range(n_dom)]
    groups = [
        [(i + h) % n_dom * n_sub + t for h in range(2) for t in range(n_sub)] for i in range(1, n_dom, 2)
    ]
    lines = [[i * n_sub + t for t in range(n_sub)] for i in range(n_dom)]
    dom = lax.axis_index("dom")
    at_end = (dom == 0) | (dom == n_dom - 1)

    def exchange(block, among):
        return lax.all_to_all(
            block, ("dom", "sub"), split_axis=0, concat_axis=0, tiled=True, axis_index_groups=among
        )

    def across_pair(block):
        return exchange(block, groups)

    def within_line(block):
        own = exchange(jnp.where(odd == 1, block[0:4], block[4:8]), lines)
        return jnp.concatenate([own, own])

    raw = [
        send_list.reshape(1, SLOTS),
        neighbour,
        stiffness,
        jnp.transpose(face_proj, (1, 0, 2)),
        face_rot,
        cluster.reshape(1, E),
        jnp.transpose(dofs, (1, 0, 2)),
        jnp.transpose(star, (1, 2, 0, 3)),
        jnp.transpose(neighbour_flux, (1, 2, 0, 3)),
        jnp.transpose(local_flux, (1, 2, 0, 3)),
        orient,
    ]
    raw = [pltpu.with_memory_space_constraint(x, pltpu.HBM) for x in raw]
    flux_s = ((NV, NV, 4, E), F32)
    constants = [
        ((4, E), jnp.int32),
        ((1, E), jnp.int32),
        ((4, E), jnp.int32),
        ((3 * NBP, 3 * NBK), BF),
        ((4 * NFP, 3 * NBK), BF),
        ((NV, NV, 3, E), F32),
        flux_s,
        flux_s,
        ((2 * NBP, 192), BF),
        ((NBP, 192), BF),
        ((NBP, 192), BF),
        ((96, FACES), BF),
        ((16, E), jnp.int32),
    ]
    terms_s = ((ORDER, NV, NBP, E), F32)
    face_s = ((2 * WIDE, FACES), BF)
    nsum_s = ((WIDE, FACES), F32)
    base_s = ((NV, NBP, E), F32)
    xs_s = ((3 * NBK, COLS), BF)
    xg_s = ((384, COLS), BF)
    xq_s = ((192, COLS), BF)
    sends = [terms_s, face_s, ((32, WIDE), F32), ((64, WIDE), F32)]
    fetched = [
        ((NV, NB, E), F32),
        ((3, NB, NB), F32),
        ((NF, 4, NB), F32),
        ((3, NF, NF), F32),
        ((1, SLOTS), jnp.int32),
        base_s,
        ((3 * NBP, NBK), F32),
        ((4 * NFP, NBK), F32),
        xs_s,
        pltpu.SemaphoreType.DMA((11,)),
    ]
    begun = call(
        opening,
        constants + sends,
        fetched,
        raw + [jnp.full((1, E), odd, jnp.int32)],
        raw=11,
    )
    neighbour, cluster, orient = begun[:3]
    stiff, proj, star, nflux, lflux, lift_a, lift_b, own_lift, pick, small = begun[3:13]
    terms, faced, p_swap, p_rest = begun[13:]
    thin_s = ((ORDER, 3, NBP, E), F32)
    thin_columns = 3 * E
    for step in range(STEPS):
        odd_step = step % 2 == 1
        if odd_step:
            fresh, faced, p_swap, p_rest = call(
                functools.partial(critical_thin, step),
                [thin_s] + sends[1:],
                [((384, thin_columns), BF), xs_s, ((3 * NBK, thin_columns), BF)],
                [came, nsum_thin, base, thin_nflux, lift_a, lift_b, small]
                + [stiff, thin_star, proj, pick, cluster, terms],
            )
        elif step > 0:
            nsum, terms, faced, p_swap, p_rest = call(
                functools.partial(critical, False, step),
                [nsum_s] + sends,
                [xg_s, xs_s],
                [came, nsum, base, nflux, lift_a, lift_b, orient, small, stiff]
                + [pair_star if step % 4 == 2 else star, proj, pick, cluster, terms],
            )
        swapped = lax.ppermute(p_swap, "dom", chip)
        side = functools.partial(beside, step)
        thin_nsum_s = ((WIDE, E), F32)
        if step == 0:
            nsum, base, nsum_thin, thin_star, thin_lflux, thin_nflux, pair_star = call(
                side,
                [nsum_s, base_s, thin_nsum_s, ((21, 3, E), F32), ((21, 4, E), F32), ((NV * NV, E), F32)]
                + [((41, 3, E), F32)],
                [xs_s, xq_s],
                [terms, faced, neighbour, stiff, star, proj, lflux, own_lift, cluster, small, nflux],
            )
        elif odd_step:
            nsum, base = call(
                side,
                [nsum_s, base_s],
                [((3 * NBK, thin_columns), BF), ((192, thin_columns), BF)],
                [fresh, faced, neighbour, stiff, thin_star, proj, thin_lflux, own_lift, cluster]
                + [small, came, nsum, base],
            )
        else:
            nsum, base, nsum_thin = call(
                side,
                [nsum_s, base_s, thin_nsum_s],
                [xs_s, xq_s],
                [terms, faced, neighbour, stiff, pair_star if step % 4 == 2 else star, proj, lflux, own_lift, cluster]
                + [small, nsum, base],
            )
        swapped = swapped.reshape(4, H, WIDE)
        block = jnp.concatenate([p_rest.reshape(8, H, WIDE), jnp.concatenate([swapped, swapped])], axis=1)
        if odd_step:
            block, nsum, base = lax.optimization_barrier((block, nsum, base))
        else:
            block, nsum, base, nsum_thin = lax.optimization_barrier((block, nsum, base, nsum_thin))
        came = lax.cond(at_end, within_line, across_pair, block).reshape(128, WIDE)
    (out,) = call(
        functools.partial(critical, True, STEPS),
        [((NV, NB, E), F32)],
        [xg_s],
        [came, nsum, base, nflux, lift_a, lift_b, orient, small],
    )
    return jnp.transpose(out, (1, 0, 2))


def solution(mesh):
    placed = (
        P(None, None, ("dom", "sub")),
        P(),
        P(None, None, None, ("dom", "sub")),
        P(None, None, None, ("dom", "sub")),
        P(None, None, None, ("dom", "sub")),
        P(),
        P(),
        P(("dom", "sub")),
        P(None, ("dom", "sub")),
        P(None, ("dom", "sub")),
        P("dom", "sub", None),
    )
    return jax.shard_map(
        body, mesh=mesh, in_specs=placed, out_specs=P(None, None, ("dom", "sub")), check_vma=False
    )
```
